128 devices in a mesh: seq: 16 (over x_hi, y, core), chan: 8 (over x_lo, z).
Axes of the slice: x: 4 (x_hi: 2, x_lo: 2; x = x_hi * 2 + x_lo), y: 4, z: 4, core: 2. Of those that a mesh axis runs over, the one named last changes fastest.
Arguments:
- out_gate: bfloat16 [4096, 8192], P('seq', 'chan'), may hold values from -6 to 6
- in_gate: bfloat16 [4096, 8192], P('seq', 'chan'), may hold values from -6 to 6
- signal: bfloat16 [4096, 8192], P('seq', 'chan'), may hold values from -6 to 6
- filter_taps: bfloat16 [4096, 8192], P('seq', 'chan'), may hold values from -5 to 5
- skip_gain: float32 [8192], P('chan'), may hold values from -4 to 4
- out_proj: bfloat16 [8192, 8192], P(None, 'chan'), may hold values from -0.09375 to 0.09375
Outputs:
- layer_out: bfloat16 [4096, 8192], P('seq', 'chan')
The draws below stay inside these ranges and needn't reach their ends.
All inputs are finite; a program needn't handle non-finite values.
Results may differ from the reference program's by a relative error of at most 0.02.
Values may be sent and summed in bfloat16 or wider, within the bound.
No kernel may reach another device: no remote copies, remote signals or barrier semaphores. Data moves between devices by JAX's collectives and lax.ppermute only.
A program may use at most 128 MiB of HBM per device.

```python
import math
import jax
import jax.numpy as jnp
from jax import lax

D = 8192
SEQ_LEN = 4096


def shared_classes(key):
    return jax.random.bernoulli(jax.random.fold_in(key, 97), 0.25, (D,))


def draw_in_gate(key, part):
    tail_mask = shared_classes(key)
    key = jax.random.fold_in(key, 11)
    noise = jnp.clip(jax.random.normal(key, (SEQ_LEN, D)), -5.0, 5.0)
    return (noise + tail_mask[None, :].astype(jnp.float32)).astype(jnp.bfloat16)


def draw_signal(key, part):
    tail_mask = shared_classes(key)
    key = jax.random.fold_in(key, 13)
    noise = jnp.clip(jax.random.normal(key, (SEQ_LEN, D)), -5.0, 5.0)
    return (noise + tail_mask[None, :].astype(jnp.float32)).astype(jnp.bfloat16)


def draw_filter_taps(key, part):
    tail_mask = shared_classes(key)
    key = jax.random.fold_in(key, 17)
    key_list = jax.random.split(key, 14)
    lag_pos = jnp.arange(SEQ_LEN, dtype=jnp.float32)[:, None]
    bump_mask = jnp.logical_and(jax.random.bernoulli(key_list[6], 0.25, (1, D)), jnp.logical_not(tail_mask[None, :]))
    fast_tau = jax.random.uniform(key_list[2], (1, D), minval=math.log(30.0), maxval=math.log(50.0))
    log_tau = jax.random.uniform(key_list[0], (1, D), minval=math.log(30.0), maxval=math.log(4.0 * SEQ_LEN))
    noise = jnp.clip(jax.random.normal(key_list[3], (SEQ_LEN, D)), -5.0, 5.0)
    log_tau = jnp.where(bump_mask, fast_tau, log_tau)
    decay_len = jnp.exp(log_tau)
    total_energy = (1.0 - jnp.exp(-2.0 * SEQ_LEN / decay_len)) / (1.0 - jnp.exp(-2.0 / decay_len))
    envelope = jnp.exp(-lag_pos / decay_len) / jnp.sqrt(total_energy)
    positions = jax.random.randint(key_list[4], (3, D), 1, SEQ_LEN)
    drops = jax.random.uniform(key_list[5], (3, D), minval=0.5, maxval=0.8)
    for index in range(3):
        envelope = envelope * jnp.where(lag_pos >= positions[index][None, :].astype(jnp.float32), drops[index][None, :], 1.0)
    bump_start = jax.random.randint(key_list[7], (1, D), SEQ_LEN // 8, SEQ_LEN - SEQ_LEN // 8).astype(jnp.float32)
    bump_tau = jnp.exp(jax.random.uniform(key_list[8], (1, D), minval=math.log(0.02 * SEQ_LEN), maxval=math.log(0.1 * SEQ_LEN)))
    bump_ratio = jax.random.uniform(key_list[9], (1, D), minval=0.7, maxval=1.4)
    bump_energy = (1.0 - jnp.exp(-2.0 * (SEQ_LEN - bump_start) / bump_tau)) / (1.0 - jnp.exp(-2.0 / bump_tau))
    after = lag_pos - bump_start
    bump_env = jnp.where(after >= 0.0, jnp.exp(-jnp.maximum(after, 0.0) / bump_tau), 0.0) * bump_ratio / jnp.sqrt(bump_energy)
    combined = jnp.where(bump_mask, (envelope + bump_env) / jnp.sqrt(1.0 + bump_ratio * bump_ratio), envelope)
    base_filter = noise * combined
    spike_size = jax.random.uniform(key_list[10], (1, D), minval=1.2, maxval=2.0)
    spike_sign = jnp.where(jax.random.bernoulli(key_list[11], 0.5, (1, D)), 1.0, -1.0)
    tail_sign = jnp.where(jax.random.bernoulli(key_list[12], 0.5, (1, D)), 1.0, -1.0)
    tail_rough = jax.random.uniform(key_list[13], (SEQ_LEN, D), minval=-0.5, maxval=2.5)
    tail_filter = jnp.where(lag_pos == 0.0, spike_size * spike_sign, tail_sign * tail_rough / SEQ_LEN)
    result = jnp.where(tail_mask[None, :], tail_filter, base_filter)
    return jnp.clip(result, -5.0, 5.0).astype(jnp.bfloat16)


def raised(values, rng, source, target, blocks, factor):
    def block_of(axis_at):
        return (jnp.arange(values.shape[axis_at]) // (values.shape[axis_at] // blocks)).reshape((-1,) + (1,) * (values.ndim - 1 - axis_at))

    near = jax.random.permutation(rng, blocks)[block_of(target)]
    second = (block_of(target) + blocks // 2) % blocks
    return jnp.where((block_of(source) == near) | (block_of(source) == second), factor * values, values)


def level_of(stream_key, extent, pieces, low, largest):
    gain, own = 1.0, jax.random.fold_in(stream_key, 6)
    for position, blocks in pieces:
        draws = jnp.exp(jax.random.uniform(jax.random.fold_in(own, position), (blocks,), jnp.float32, low / len(pieces), largest / len(pieces)))
        gain = gain * jnp.repeat(draws, extent[position] // blocks).reshape([-1 if axis == position else 1 for axis in range(len(extent))])
    return gain


def centred(own_key, dims, scale, reach, cuts=(), kind=jnp.bfloat16):
    drawn = scale * jax.random.normal(own_key, dims, jnp.float32)
    if cuts:
        drawn = drawn * level_of(own_key, dims, cuts, -0.22, 0.18)
    return jnp.clip(drawn, -reach, reach).astype(kind)


def gaussian_with(own_key, shape, spread, limit, pieces, heavy, kind=jnp.bfloat16):
    array = spread * jax.random.normal(own_key, shape, jnp.float32)
    if pieces:
        array = array * level_of(own_key, shape, pieces, -0.22, 0.18)
    return jnp.clip(raised(array, jax.random.fold_in(own_key, 3), *heavy), -limit, limit).astype(kind)


def setup_inputs(seed: int = 0) -> dict:
    splits = jax.random.split(jax.random.key(seed), 7)
    out_gate = centred(splits[0], (SEQ_LEN, D), 1.0, 6.0, ((0, 16), (1, 8)))
    in_gate = draw_in_gate(jax.random.fold_in(splits[6], 71), 0)
    signal = draw_signal(jax.random.fold_in(splits[6], 71), 0)
    filter_taps = draw_filter_taps(jax.random.fold_in(splits[6], 71), 0)
    skip_gain = centred(splits[4], (D,), 1.0, 4.0, ((0, 8),), jnp.float32)
    out_proj = gaussian_with(splits[5], (D, D), D ** -0.5, 0.09375, ((1, 8),), (1, 0, 8, 2.0))
    return {"out_gate": out_gate, "in_gate": in_gate, "signal": signal, "filter_taps": filter_taps, "skip_gain": skip_gain, "out_proj": out_proj}


def reference(out_gate, in_gate, signal, filter_taps, skip_gain, out_proj):
    gated_rows = (in_gate.astype(jnp.float32) * signal.astype(jnp.float32)).astype(jnp.bfloat16)
    block_width = 128
    block_count = D // block_width
    fft_size = 2 * SEQ_LEN

    def convolve(block_pair):
        source, tap_rows = block_pair
        source_spec = jnp.fft.rfft(source, n=fft_size, axis=0)
        filter_spec = jnp.fft.rfft(tap_rows, n=fft_size, axis=0)
        return jnp.fft.irfft(source_spec * filter_spec, n=fft_size, axis=0)[:SEQ_LEN]

    source_blocks = gated_rows.astype(jnp.float32).reshape(SEQ_LEN, block_count, block_width).transpose(1, 0, 2)
    tap_blocks = filter_taps.astype(jnp.float32).reshape(SEQ_LEN, block_count, block_width).transpose(1, 0, 2)
    conv_rows = lax.map(convolve, (source_blocks, tap_blocks))
    conv_rows = conv_rows.transpose(1, 0, 2).reshape(SEQ_LEN, D)
    mixed_rows = (out_gate.astype(jnp.float32) * (conv_rows + skip_gain[None, :] * gated_rows.astype(jnp.float32))).astype(jnp.bfloat16)
    return jnp.dot(mixed_rows, out_proj.T, preferred_element_type=jnp.float32).astype(jnp.bfloat16)
```

```python
import numpy as np

import jax
import jax.numpy as jnp
from jax import lax
from jax.experimental import pallas as pl
from jax.experimental.pallas import tpu as pltpu
from jax.sharding import PartitionSpec as P

F32, BF16 = jnp.float32, jnp.bfloat16


def split_bf16(table):
    high = table.astype(BF16)
    low = (table - high.astype(np.float64)).astype(BF16)
    return high, low


def transform_tables(n):
    freq = np.arange(n, dtype=np.float64) + 0.5
    angle = np.pi / n * np.outer(np.arange(n, dtype=np.float64), freq)
    forward = np.concatenate([np.cos(angle), -np.sin(angle)], axis=1)
    inverse = np.concatenate([np.cos(angle).T, -np.sin(angle).T], axis=0) / n
    return split_bf16(forward) + split_bf16(inverse)


def prepare_kernel(in_gate, signal, taps, out_gate, packed, out_gate_t):
    gated = (in_gate[...].astype(F32) * signal[...].astype(F32)).astype(BF16)
    parts, both, tokens = packed.shape
    half = both // 2
    packed[:, :half, :] = gated.T.reshape(parts, half, tokens)
    packed[:, half:, :] = taps[...].T.reshape(parts, half, tokens)
    out_gate_t[...] = out_gate[...].T


def prepare(in_gate, signal, taps, out_gate, parts):
    tokens, channels = in_gate.shape
    per_part = channels // parts
    wide = 128
    block = pl.BlockSpec((tokens, wide), lambda i: (0, i))
    return pl.pallas_call(
        prepare_kernel,
        grid=(channels // wide,),
        in_specs=[block] * 4,
        out_specs=[
            pl.BlockSpec((wide // per_part, 2 * per_part, tokens), lambda i: (i, 0, 0)),
            pl.BlockSpec((wide, tokens), lambda i: (i, 0)),
        ],
        out_shape=[
            jax.ShapeDtypeStruct((parts, 2 * per_part, tokens), BF16),
            jax.ShapeDtypeStruct((channels, tokens), BF16),
        ],
        name="prepare",
    )(in_gate, signal, taps, out_gate)


def conv_kernel(packed, fwd_high, fwd_low, inv_high, inv_low, skip, out, g_spec, p_spec, acc_high, acc_low):
    blocks, both, n = packed.shape
    ch = both // 2
    lane = lax.broadcasted_iota(jnp.int32, (1, n), 1)
    sign = jnp.where(lane % 2 == 0, 1.0, -1.0).astype(F32)

    def transform(rows):
        return jnp.dot(rows, fwd_high[...], preferred_element_type=F32) + jnp.dot(
            rows, fwd_low[...], preferred_element_type=F32
        )

    group = 4
    tail = None
    for b in range(0, blocks, group):
        rows = packed[b : b + group]
        g_spec[b : b + group] = transform(rows[:, :ch].reshape(group * ch, n)).reshape(group, ch, 2 * n)
        h = transform(rows[:, ch:].reshape(group * ch, n)).reshape(group, ch, 2 * n)
        for j in range(group):
            if tail is None:
                p_spec[b + j] = h[j]
            else:
                p_spec[b + j, :, :n] = h[j, :, :n] - sign * tail[:, n:]
                p_spec[b + j, :, n:] = h[j, :, n:] + sign * tail[:, :n]
            tail = h[j]

    lanes, subs = 128, 16

    def products(step, carry):
        rows = pl.ds(pl.multiple_of(step * subs, subs), subs)
        for f in range(0, n, lanes):
            re, im = slice(f, f + lanes), slice(n + f, n + f + lanes)
            for i in range(blocks):
                acc_re = acc_im = None
                for a in range(i + 1):
                    gr, gi = g_spec[a, rows, re], g_spec[a, rows, im]
                    pr, pi = p_spec[i - a, rows, re], p_spec[i - a, rows, im]
                    t_re, t_im = gr * pr - gi * pi, gr * pi + gi * pr
                    acc_re = t_re if acc_re is None else acc_re + t_re
                    acc_im = t_im if acc_im is None else acc_im + t_im
                for value, cols in ((acc_re, re), (acc_im, im)):
                    high = value.astype(BF16)
                    acc_high[i, rows, cols] = high
                    acc_low[i, rows, cols] = (value - high.astype(F32)).astype(BF16)
        return carry

    lax.fori_loop(0, ch // subs, products, 0)

    for b in range(0, blocks, group):
        high = acc_high[b : b + group].reshape(group * ch, 2 * n)
        low = acc_low[b : b + group].reshape(group * ch, 2 * n)
        conv = (
            jnp.dot(high, inv_high[...], preferred_element_type=F32)
            + jnp.dot(low, inv_high[...], preferred_element_type=F32)
            + jnp.dot(high, inv_low[...], preferred_element_type=F32)
        ).reshape(group, ch, n)
        gated = packed[b : b + group, :ch, :].astype(F32)
        out[b : b + group] = (conv + skip[...][None] * gated).astype(BF16)


def convolve(packed, skip):
    blocks, both, n = packed.shape
    ch = both // 2
    tables = transform_tables(n)
    return pl.pallas_call(
        conv_kernel,
        in_specs=[pl.BlockSpec(memory_space=pltpu.VMEM)] * 6,
        out_specs=pl.BlockSpec(memory_space=pltpu.VMEM),
        out_shape=jax.ShapeDtypeStruct((blocks, ch, n), BF16),
        scratch_shapes=[
            pltpu.VMEM((blocks, ch, 2 * n), F32),
            pltpu.VMEM((blocks, ch, 2 * n), F32),
            pltpu.VMEM((blocks, ch, 2 * n), BF16),
            pltpu.VMEM((blocks, ch, 2 * n), BF16),
        ],
        compiler_params=pltpu.CompilerParams(vmem_limit_bytes=40 * 2**20),
        name="convolve",
    )(packed, *(jnp.asarray(t) for t in tables), skip)


def shards(out_gate, in_gate, signal, filter_taps, skip_gain, out_proj):
    tokens, channels = out_gate.shape
    parts, chans = lax.axis_size("seq"), lax.axis_size("chan")
    per_part = channels // parts
    packed, out_gate_t = prepare(in_gate, signal, filter_taps, out_gate, parts)
    packed = lax.all_to_all(packed, "seq", 0, 0)
    skip = lax.dynamic_slice_in_dim(skip_gain, lax.axis_index("seq") * per_part, per_part, 0)
    conv = convolve(packed, skip[:, None])
    conv = lax.all_to_all(conv, "seq", 0, 0).reshape(channels, tokens)
    mixed = (out_gate_t.astype(F32) * conv.astype(F32)).astype(BF16)
    partial = jnp.dot(out_proj, mixed, preferred_element_type=F32).astype(BF16)
    shares = lax.all_to_all(partial.reshape(chans, -1, tokens), "chan", 0, 0)
    return jnp.sum(shares.astype(F32), axis=0).T.astype(BF16)


def solution(mesh):
    return jax.shard_map(
        shards,
        mesh=mesh,
        in_specs=(
            P("seq", "chan"),
            P("seq", "chan"),
            P("seq", "chan"),
            P("seq", "chan"),
            P("chan"),
            P(None, "chan"),
        ),
        out_specs=P("seq", "chan"),
        check_vma=False,
    )
```

```python
import numpy as np

import jax
import jax.numpy as jnp
from jax import lax
from jax.experimental import pallas as pl
from jax.experimental.pallas import tpu as pltpu
from jax.sharding import PartitionSpec as P

F32, BF16 = jnp.float32, jnp.bfloat16


def split_bf16(table):
    high = table.astype(BF16)
    low = (table - high.astype(np.float64)).astype(BF16)
    return high, low


def transform_table(n):
    freq = np.arange(n, dtype=np.float64) + 0.5
    angle = np.pi / n * np.outer(np.arange(n, dtype=np.float64), freq)
    forward = np.concatenate([np.cos(angle), -np.sin(angle)], axis=1)
    high, low = split_bf16(forward)
    return np.concatenate([high, low], axis=0)


def prepare_kernel(in_gate, signal, taps, out_gate, packed, out_gate_t):
    gated = (in_gate[...].astype(F32) * signal[...].astype(F32)).astype(BF16)
    parts, both, tokens = packed.shape
    half = both // 2
    packed[:, :half, :] = gated.T.reshape(parts, half, tokens)
    packed[:, half:, :] = taps[...].T.reshape(parts, half, tokens)
    out_gate_t[...] = out_gate[...].T


def prepare(in_gate, signal, taps, out_gate, parts):
    tokens, channels = in_gate.shape
    per_part = channels // parts
    wide = 128
    block = pl.BlockSpec((tokens, wide), lambda i: (0, i))
    return pl.pallas_call(
        prepare_kernel,
        grid=(channels // wide,),
        in_specs=[block] * 4,
        out_specs=[
            pl.BlockSpec((wide // per_part, 2 * per_part, tokens), lambda i: (i, 0, 0)),
            pl.BlockSpec((wide, tokens), lambda i: (i, 0)),
        ],
        out_shape=[
            jax.ShapeDtypeStruct((parts, 2 * per_part, tokens), BF16),
            jax.ShapeDtypeStruct((channels, tokens), BF16),
        ],
        name="prepare",
    )(in_gate, signal, taps, out_gate)


def conv_kernel(packed, table, skip, out, g_spec, p_spec, acc_high, acc_low):
    blocks, both, n = packed.shape
    ch = both // 2
    lane = lax.broadcasted_iota(jnp.int32, (1, n), 1)
    sign = jnp.where(lane % 2 == 0, 1.0, -1.0).astype(F32)

    def transform(rows):
        return jnp.dot(rows, table[:n], preferred_element_type=F32) + jnp.dot(
            rows, table[n:], preferred_element_type=F32
        )

    def inverse(spectra, part):
        return lax.dot_general(spectra, part, (((1,), (1,)), ((), ())), preferred_element_type=F32)

    group = 4
    tail = None
    for b in range(0, blocks, group):
        rows = packed[b : b + group]
        g_spec[b : b + group] = transform(rows[:, :ch].reshape(group * ch, n)).reshape(group, ch, 2 * n)
        h = transform(rows[:, ch:].reshape(group * ch, n)).reshape(group, ch, 2 * n)
        for j in range(group):
            if tail is None:
                p_spec[b + j] = h[j]
            else:
                p_spec[b + j, :, :n] = h[j, :, :n] - sign * tail[:, n:]
                p_spec[b + j, :, n:] = h[j, :, n:] + sign * tail[:, :n]
            tail = h[j]

    lanes, subs = 128, 16

    def products(step, carry):
        rows = pl.ds(pl.multiple_of(step * subs, subs), subs)
        for f in range(0, n, lanes):
            re, im = slice(f, f + lanes), slice(n + f, n + f + lanes)
            for i in range(blocks):
                acc_re = acc_im = None
                for a in range(i + 1):
                    gr, gi = g_spec[a, rows, re], g_spec[a, rows, im]
                    pr, pi = p_spec[i - a, rows, re], p_spec[i - a, rows, im]
                    t_re, t_im = gr * pr - gi * pi, gr * pi + gi * pr
                    acc_re = t_re if acc_re is None else acc_re + t_re
                    acc_im = t_im if acc_im is None else acc_im + t_im
                for value, cols in ((acc_re, re), (acc_im, im)):
                    high = value.astype(BF16)
                    acc_high[i, rows, cols] = high
                    acc_low[i, rows, cols] = (value - high.astype(F32)).astype(BF16)
        return carry

    lax.fori_loop(0, ch // subs, products, 0)

    for b in range(0, blocks, group):
        high = acc_high[b : b + group].reshape(group * ch, 2 * n)
        low = acc_low[b : b + group].reshape(group * ch, 2 * n)
        conv = inverse(high, table[:n]) + inverse(low, table[:n]) + inverse(high, table[n:])
        conv = (conv * (1.0 / n)).reshape(group, ch, n)
        gated = packed[b : b + group, :ch, :].astype(F32)
        out[b : b + group] = (conv + skip[...][None] * gated).astype(BF16)


def convolve(packed, skip):
    blocks, both, n = packed.shape
    ch = both // 2
    return pl.pallas_call(
        conv_kernel,
        in_specs=[pl.BlockSpec(memory_space=pltpu.VMEM)] * 3,
        out_specs=pl.BlockSpec(memory_space=pltpu.VMEM),
        out_shape=jax.ShapeDtypeStruct((blocks, ch, n), BF16),
        scratch_shapes=[
            pltpu.VMEM((blocks, ch, 2 * n), F32),
            pltpu.VMEM((blocks, ch, 2 * n), F32),
            pltpu.VMEM((blocks, ch, 2 * n), BF16),
            pltpu.VMEM((blocks, ch, 2 * n), BF16),
        ],
        compiler_params=pltpu.CompilerParams(vmem_limit_bytes=40 * 2**20),
        name="convolve",
    )(packed, jnp.asarray(transform_table(n)), skip)


def project_kernel(order, weight, gate, conv, out, mixed):
    @pl.when(pl.program_id(0) == 0)
    def _():
        mixed[...] = (gate[...].astype(F32) * conv[...].astype(F32)).astype(BF16)

    out[0] = jnp.dot(weight[...], mixed[...], preferred_element_type=F32).astype(BF16)


def project(weight, gate, conv, starts, rows):
    channels, tokens = conv.shape
    count = len(starts)
    whole = pl.BlockSpec((channels, tokens), lambda i, order: (0, 0))
    return pl.pallas_call(
        project_kernel,
        grid_spec=pltpu.PrefetchScalarGridSpec(
            num_scalar_prefetch=1,
            grid=(count,),
            in_specs=[
                pl.BlockSpec((pl.Element(rows), pl.Element(channels)), lambda i, order: (pl.multiple_of(order[i], 16), 0)),
                whole,
                whole,
            ],
            out_specs=pl.BlockSpec((1, rows, tokens), lambda i, order: (i, 0, 0)),
            scratch_shapes=[pltpu.VMEM((channels, tokens), BF16)],
        ),
        out_shape=jax.ShapeDtypeStruct((count, rows, tokens), BF16),
        cost_estimate=pl.CostEstimate(
            flops=2 * count * rows * channels * tokens,
            bytes_accessed=2 * (count * rows * (channels + tokens) + 2 * channels * tokens),
            transcendentals=0,
        ),
        name="project",
    )(jnp.stack(starts).astype(jnp.int32), weight, gate, conv)


Z = 4


def to_z(block, step):
    n = lax.axis_size("chan")
    return lax.ppermute(block, "chan", [(i, i // Z * Z + (i + step) % Z) for i in range(n)])


def to_other_x(block):
    n = lax.axis_size("chan")
    return lax.ppermute(block, "chan", [(i, (i + Z) % n) for i in range(n)])


def reduce_z(plus, minus, keep_plus, keep_minus, own_first, own_second):
    from_below, from_above = to_z(plus, 1), to_z(minus, -1)
    k = keep_plus.shape[0]
    up = to_z((keep_plus.astype(F32) + from_below[:k].astype(F32)).astype(BF16), 1)
    down = to_z((keep_minus.astype(F32) + from_above[:k].astype(F32)).astype(BF16), -1)
    first = own_first.astype(F32) + from_above[k:].astype(F32) + up.astype(F32)
    second = own_second.astype(F32) + from_below[k:].astype(F32) + down.astype(F32)
    return first, second


def shards(out_gate, in_gate, signal, filter_taps, skip_gain, out_proj):
    tokens, channels = out_gate.shape
    parts, chans = lax.axis_size("seq"), lax.axis_size("chan")
    per_part = channels // parts
    packed, out_gate_t = prepare(in_gate, signal, filter_taps, out_gate, parts)
    packed = lax.all_to_all(packed, "seq", 0, 0)
    skip = lax.dynamic_slice_in_dim(skip_gain, lax.axis_index("seq") * per_part, per_part, 0)
    conv = convolve(packed, skip[:, None])
    conv = lax.all_to_all(conv, "seq", 0, 0).reshape(channels, tokens)

    me = lax.axis_index("chan")
    x, z = me // Z, me % Z
    chunk = out_proj.shape[0] // chans
    half_a = 192
    half_b = chunk // 2 - half_a

    def at(flip, step, offset):
        return (((x + flip) % 2) * Z + (z + step) % Z) * chunk + offset

    a1, a2, b1, b2 = 0, half_a, 2 * half_a, 2 * half_a + half_b
    order = [(2, 0), (1, 1), (2, 1), (3, 0), (1, 0), (3, 1), (0, 0), (0, 1)]
    rows_a = lambda flip: [at(flip, s, (a1, a2)[h]) for s, h in order]
    rows_b = [at(flip, s, (b1, b2)[h]) for s, h in order for flip in (0, 1)]
    run = lambda starts, rows: project(out_proj, out_gate_t, conv, starts, rows)

    from_x = to_other_x(run(rows_a(1), half_a))
    plus_b = run(rows_b[:4], half_b)
    minus_b = run(rows_b[4:8], half_b)
    rest_b = run(rows_b[8:], half_b)
    own_a = run(rows_a(0), half_a)

    def summed_a(lo, hi):
        return own_a[lo:hi].astype(F32) + from_x[lo:hi].astype(F32)

    b_first, b_second = reduce_z(plus_b, minus_b, rest_b[:2], rest_b[2:4], rest_b[4:6], rest_b[6:8])
    other_b = to_other_x(jnp.stack([b_first[1], b_second[1]]).astype(BF16)).astype(F32)
    a_first, a_second = reduce_z(
        summed_a(0, 2).astype(BF16), summed_a(2, 4).astype(BF16),
        summed_a(4, 5), summed_a(5, 6), summed_a(6, 7), summed_a(7, 8),
    )
    rows = [a_first[0], a_second[0], b_first[0] + other_b[0], b_second[0] + other_b[1]]
    return jnp.concatenate([r.astype(BF16) for r in rows], axis=0).T


def solution(mesh):
    return jax.shard_map(
        shards,
        mesh=mesh,
        in_specs=(
            P("seq", "chan"),
            P("seq", "chan"),
            P("seq", "chan"),
            P("seq", "chan"),
            P("chan"),
            P(None, "chan"),
        ),
        out_specs=P("seq", "chan"),
        check_vma=False,
    )
```

```python
import functools

import numpy as np

import jax
import jax.numpy as jnp
from jax import lax
from jax.experimental import pallas as pl
from jax.experimental.pallas import tpu as pltpu
from jax.sharding import PartitionSpec as P

F32, BF16 = jnp.float32, jnp.bfloat16


def split_bf16(table):
    high = table.astype(BF16)
    low = (table - high.astype(np.float64)).astype(BF16)
    return high, low


def transform_table(n):
    freq = np.arange(n, dtype=np.float64) + 0.5
    angle = np.pi / n * np.outer(np.arange(n, dtype=np.float64), freq)
    forward = np.concatenate([np.cos(angle), -np.sin(angle)], axis=1)
    high, low = split_bf16(forward)
    inverse = [part.T.astype(np.float64) / n for part in (high, low)]
    return np.concatenate([high, low, np.concatenate(inverse, axis=1).astype(BF16)], axis=0)


def prepare_kernel(in_gate, signal, taps, packed, gate_buf, signal_buf, taps_buf, sems):
    parts, both, tokens = packed.shape
    half = both // 2
    steps, wide = gate_buf.shape[0], gate_buf.shape[2]
    copies = [
        [
            pltpu.make_async_copy(source.at[:, i * wide : (i + 1) * wide], buf.at[i], sems.at[i, j])
            for j, (source, buf) in enumerate(((in_gate, gate_buf), (signal, signal_buf), (taps, taps_buf)))
        ]
        for i in range(steps)
    ]
    for step in copies:
        for copy in step:
            copy.start()
    count = wide // half
    for i, step in enumerate(copies):
        for copy in step:
            copy.wait()
        gated = (gate_buf[i].astype(F32) * signal_buf[i].astype(F32)).astype(BF16)
        packed[i * count : (i + 1) * count, :half] = gated.T.reshape(count, half, tokens)
        packed[i * count : (i + 1) * count, half:] = taps_buf[i].T.reshape(count, half, tokens)


def prepare(in_gate, signal, taps, parts):
    tokens, channels = in_gate.shape
    steps = 4
    wide = channels // steps
    return pl.pallas_call(
        prepare_kernel,
        in_specs=[pl.BlockSpec(memory_space=pltpu.HBM)] * 3,
        out_specs=pl.BlockSpec(memory_space=pltpu.VMEM),
        out_shape=jax.ShapeDtypeStruct((parts, 2 * channels // parts, tokens), BF16),
        scratch_shapes=[pltpu.VMEM((steps, tokens, wide), BF16)] * 3 + [pltpu.SemaphoreType.DMA((steps, 3))],
        compiler_params=pltpu.CompilerParams(vmem_limit_bytes=60 * 2**20),
        name="prepare",
    )(in_gate, signal, taps)


def conv_kernel(
    packed, skip, table_far, gate_far, weight_far, out, gate_t, weight, table, gate, g_spec, p_spec, acc_high, acc_low, sems
):
    copies = [
        pltpu.make_async_copy(source, target, sems.at[i])
        for i, (source, target) in enumerate(((table_far, table), (gate_far, gate), (weight_far, weight)))
    ]
    for copy in copies:
        copy.start()
    copies[0].wait()
    copies[1].wait()
    gate_t[...] = gate[...].T
    blocks, both, n = packed.shape
    ch = both // 2
    lane = lax.broadcasted_iota(jnp.int32, (1, n), 1)
    sign = jnp.where(lane % 2 == 0, 1.0, -1.0).astype(F32)

    def transform(rows):
        return jnp.dot(rows, table[:n], preferred_element_type=F32) + jnp.dot(
            rows, table[n : 2 * n], preferred_element_type=F32
        )

    def inverse(spectra, part):
        return jnp.dot(spectra, table[2 * n :, part * n : (part + 1) * n], preferred_element_type=F32)

    group = 4
    tail = None
    for b in range(0, blocks, group):
        rows = packed[b : b + group]
        g_spec[b : b + group] = transform(rows[:, :ch].reshape(group * ch, n)).reshape(group, ch, 2 * n)
        h = transform(rows[:, ch:].reshape(group * ch, n)).reshape(group, ch, 2 * n)
        for j in range(group):
            if tail is None:
                p_spec[b + j] = h[j]
            else:
                p_spec[b + j, :, :n] = h[j, :, :n] - sign * tail[:, n:]
                p_spec[b + j, :, n:] = h[j, :, n:] + sign * tail[:, :n]
            tail = h[j]

    lanes, subs = 128, 16

    def products(step, carry):
        rows = pl.ds(pl.multiple_of(step * subs, subs), subs)
        for f in range(0, n, lanes):
            re, im = slice(f, f + lanes), slice(n + f, n + f + lanes)
            for i in range(blocks):
                acc_re = acc_im = None
                for a in range(i + 1):
                    gr, gi = g_spec[a, rows, re], g_spec[a, rows, im]
                    pr, pi = p_spec[i - a, rows, re], p_spec[i - a, rows, im]
                    t_re, t_im = gr * pr - gi * pi, gr * pi + gi * pr
                    acc_re = t_re if acc_re is None else acc_re + t_re
                    acc_im = t_im if acc_im is None else acc_im + t_im
                for value, cols in ((acc_re, re), (acc_im, im)):
                    high = value.astype(BF16)
                    acc_high[i, rows, cols] = high
                    acc_low[i, rows, cols] = (value - high.astype(F32)).astype(BF16)
        return carry

    lax.fori_loop(0, ch // subs, products, 0)

    for b in range(0, blocks, group):
        high = acc_high[b : b + group].reshape(group * ch, 2 * n)
        low = acc_low[b : b + group].reshape(group * ch, 2 * n)
        conv = (inverse(high, 0) + inverse(low, 0) + inverse(high, 1)).reshape(group, ch, n)
        gated = packed[b : b + group, :ch, :].astype(F32)
        out[b : b + group] = (conv + skip[...][None] * gated).astype(BF16)
    copies[2].wait()


def convolve(packed, skip, table, gate, weight):
    blocks, both, n = packed.shape
    ch = both // 2
    near, far = pl.BlockSpec(memory_space=pltpu.VMEM), pl.BlockSpec(memory_space=pltpu.HBM)
    return pl.pallas_call(
        conv_kernel,
        in_specs=[near, near, far, far, far],
        out_specs=[near] * 3,
        out_shape=[
            jax.ShapeDtypeStruct((blocks, ch, n), BF16),
            jax.ShapeDtypeStruct(gate.shape[::-1], BF16),
            jax.ShapeDtypeStruct(weight.shape, BF16),
        ],
        scratch_shapes=[
            pltpu.VMEM(table.shape, BF16),
            pltpu.VMEM(gate.shape, BF16),
            pltpu.VMEM((blocks, ch, 2 * n), F32),
            pltpu.VMEM((blocks, ch, 2 * n), F32),
            pltpu.VMEM((blocks, ch, 2 * n), BF16),
            pltpu.VMEM((blocks, ch, 2 * n), BF16),
            pltpu.SemaphoreType.DMA((3,)),
        ],
        compiler_params=pltpu.CompilerParams(vmem_limit_bytes=28 * 2**20),
        name="convolve",
    )(packed, skip, table, gate, weight)


def project_kernel(weight, mixed, out, *, pieces, chunk):
    me = lax.axis_index("chan")
    rows = out.shape[1]
    for i, (flip, step, offset) in enumerate(pieces):
        start = ((me // Z + flip) % 2 * Z + (me % Z + step) % Z) * chunk + offset
        block = weight[pl.ds(pl.multiple_of(start, 16), rows), :]
        out[i] = jnp.dot(block, mixed[...], preferred_element_type=F32).astype(BF16)


def project(weight, mixed, pieces, rows, chunk):
    channels, tokens = mixed.shape
    count = len(pieces)
    in_vmem = pl.BlockSpec(memory_space=pltpu.VMEM)
    return pl.pallas_call(
        functools.partial(project_kernel, pieces=pieces, chunk=chunk),
        in_specs=[in_vmem] * 2,
        out_specs=in_vmem,
        out_shape=jax.ShapeDtypeStruct((count, rows, tokens), BF16),
        compiler_params=pltpu.CompilerParams(vmem_limit_bytes=8 * 2**20),
        cost_estimate=pl.CostEstimate(
            flops=2 * count * rows * channels * tokens,
            bytes_accessed=2 * count * rows * tokens,
            transcendentals=0,
        ),
        name="project",
    )(weight, mixed)


Z = 4


def to_z(block, step):
    n = lax.axis_size("chan")
    return lax.ppermute(block, "chan", [(i, i // Z * Z + (i + step) % Z) for i in range(n)])


def to_other_x(block):
    n = lax.axis_size("chan")
    return lax.ppermute(block, "chan", [(i, (i + Z) % n) for i in range(n)])


def reduce_z(plus, minus, keep_plus, keep_minus, own_first, own_second):
    from_below, from_above = to_z(plus, 1), to_z(minus, -1)
    k = keep_plus.shape[0]
    up = to_z((keep_plus.astype(F32) + from_below[:k].astype(F32)).astype(BF16), 1)
    down = to_z((keep_minus.astype(F32) + from_above[:k].astype(F32)).astype(BF16), -1)
    first = own_first.astype(F32) + from_above[k:].astype(F32) + up.astype(F32)
    second = own_second.astype(F32) + from_below[k:].astype(F32) + down.astype(F32)
    return first, second


def shards(out_gate, in_gate, signal, filter_taps, skip_gain, out_proj):
    tokens, channels = out_gate.shape
    parts, chans = lax.axis_size("seq"), lax.axis_size("chan")
    per_part = channels // parts
    packed = prepare(in_gate, signal, filter_taps, parts)
    packed = lax.all_to_all(packed, "seq", 0, 0)
    skip = lax.dynamic_slice_in_dim(skip_gain, lax.axis_index("seq") * per_part, per_part, 0)
    table = jnp.asarray(transform_table(tokens))
    conv, out_gate_t, out_proj = convolve(packed, skip[:, None], table, out_gate, out_proj)
    conv = lax.all_to_all(conv, "seq", 0, 0).reshape(channels, tokens)

    mixed = (out_gate_t.astype(F32) * conv.astype(F32)).astype(BF16)
    chunk = out_proj.shape[0] // chans
    half_a = 192
    half_b = chunk // 2 - half_a
    order = [(2, 0), (1, 1), (2, 1), (3, 0), (1, 0), (3, 1), (0, 0), (0, 1)]
    rows_a = [[(flip, s, h * half_a) for s, h in order] for flip in (0, 1)]
    rows_b = [(flip, s, 2 * half_a + h * half_b) for s, h in order for flip in (0, 1)]

    from_x = to_other_x(project(out_proj, mixed, rows_a[1], half_a, chunk))
    plus_b = project(out_proj, mixed, rows_b[:4], half_b, chunk)
    minus_b = project(out_proj, mixed, rows_b[4:8], half_b, chunk)
    own_a = project(out_proj, mixed, rows_a[0], half_a, chunk)
    rest_b = project(out_proj, mixed, rows_b[8:], half_b, chunk)

    def summed_a(lo, hi):
        return own_a[lo:hi].astype(F32) + from_x[lo:hi].astype(F32)

    b_first, b_second = reduce_z(plus_b, minus_b, rest_b[:2], rest_b[2:4], rest_b[4:6], rest_b[6:8])
    other_b = to_other_x(jnp.stack([b_first[1], b_second[1]]).astype(BF16)).astype(F32)
    a_first, a_second = reduce_z(
        summed_a(0, 2).astype(BF16), summed_a(2, 4).astype(BF16),
        summed_a(4, 5), summed_a(5, 6), summed_a(6, 7), summed_a(7, 8),
    )
    rows = [a_first[0], a_second[0], b_first[0] + other_b[0], b_second[0] + other_b[1]]
    return jnp.concatenate([r.astype(BF16) for r in rows], axis=0).T


def solution(mesh):
    return jax.shard_map(
        shards,
        mesh=mesh,
        in_specs=(
            P("seq", "chan"),
            P("seq", "chan"),
            P("seq", "chan"),
            P("seq", "chan"),
            P("chan"),
            P(None, "chan"),
        ),
        out_specs=P("seq", "chan"),
        check_vma=False,
    )
```

```python
import numpy as np

import jax
import jax.numpy as jnp
from jax import lax
from jax.experimental import pallas as pl
from jax.experimental.pallas import tpu as pltpu
from jax.sharding import PartitionSpec as P

F32, BF16 = jnp.float32, jnp.bfloat16


def split_bf16(table):
    high = table.astype(BF16)
    low = (table - high.astype(np.float64)).astype(BF16)
    return high, low


def transform_table(n):
    freq = np.arange(n, dtype=np.float64) + 0.5
    angle = np.pi / n * np.outer(np.arange(n, dtype=np.float64), freq)
    forward = np.concatenate([np.cos(angle), -np.sin(angle)], axis=1)
    high, low = split_bf16(forward)
    inverse = [part.T.astype(np.float64) / n for part in (high, low)]
    return np.concatenate([high, low, np.concatenate(inverse, axis=1).astype(BF16)], axis=0)


def prepare_kernel(in_gate, signal, taps, packed, gate_buf, signal_buf, taps_buf, sems):
    parts, both, tokens = packed.shape
    half = both // 2
    steps, wide = gate_buf.shape[0], gate_buf.shape[2]
    copies = [
        [
            pltpu.make_async_copy(source.at[:, i * wide : (i + 1) * wide], buf.at[i], sems.at[i, j])
            for j, (source, buf) in enumerate(((in_gate, gate_buf), (signal, signal_buf), (taps, taps_buf)))
        ]
        for i in range(steps)
    ]
    for step in copies:
        for copy in step:
            copy.start()
    count = wide // half
    for i, step in enumerate(copies):
        for copy in step:
            copy.wait()
        gated = (gate_buf[i].astype(F32) * signal_buf[i].astype(F32)).astype(BF16)
        packed[i * count : (i + 1) * count, :half] = gated.T.reshape(count, half, tokens)
        packed[i * count : (i + 1) * count, half:] = taps_buf[i].T.reshape(count, half, tokens)


def prepare(in_gate, signal, taps, parts):
    tokens, channels = in_gate.shape
    steps = 4
    wide = channels // steps
    return pl.pallas_call(
        prepare_kernel,
        in_specs=[pl.BlockSpec(memory_space=pltpu.HBM)] * 3,
        out_specs=pl.BlockSpec(memory_space=pltpu.VMEM),
        out_shape=jax.ShapeDtypeStruct((parts, 2 * channels // parts, tokens), BF16),
        scratch_shapes=[pltpu.VMEM((steps, tokens, wide), BF16)] * 3 + [pltpu.SemaphoreType.DMA((steps, 3))],
        compiler_params=pltpu.CompilerParams(vmem_limit_bytes=60 * 2**20),
        name="prepare",
    )(in_gate, signal, taps)


def conv_kernel(
    packed, skip, gate_other, table_far, gate_far, weight_far, out, gate_t, weight, table, gate, g_spec, p_spec, acc_high, acc_low, sems
):
    copies = [
        pltpu.make_async_copy(source, target, sems.at[i])
        for i, (source, target) in enumerate(((table_far, table), (gate_far, gate), (weight_far, weight)))
    ]
    for copy in copies:
        copy.start()
    copies[0].wait()
    copies[1].wait()
    blocks, both, n = packed.shape
    gate_t[:, :n] = gate[...].T
    gate_t[:, n:] = gate_other[...].T
    ch = both // 2
    lane = lax.broadcasted_iota(jnp.int32, (1, n), 1)
    sign = jnp.where(lane % 2 == 0, 1.0, -1.0).astype(F32)

    def transform(rows):
        return jnp.dot(rows, table[:n], preferred_element_type=F32) + jnp.dot(
            rows, table[n : 2 * n], preferred_element_type=F32
        )

    def inverse(spectra, part):
        return jnp.dot(spectra, table[2 * n :, part * n : (part + 1) * n], preferred_element_type=F32)

    group = 4
    tail = None
    for b in range(0, blocks, group):
        rows = packed[b : b + group]
        g_spec[b : b + group] = transform(rows[:, :ch].reshape(group * ch, n)).reshape(group, ch, 2 * n)
        h = transform(rows[:, ch:].reshape(group * ch, n)).reshape(group, ch, 2 * n)
        for j in range(group):
            if tail is None:
                p_spec[b + j] = h[j]
            else:
                p_spec[b + j, :, :n] = h[j, :, :n] - sign * tail[:, n:]
                p_spec[b + j, :, n:] = h[j, :, n:] + sign * tail[:, :n]
            tail = h[j]

    lanes, subs = 128, 16

    def products(step, carry):
        rows = pl.ds(pl.multiple_of(step * subs, subs), subs)
        for f in range(0, n, lanes):
            re, im = slice(f, f + lanes), slice(n + f, n + f + lanes)
            for i in range(blocks):
                acc_re = acc_im = None
                for a in range(i + 1):
                    gr, gi = g_spec[a, rows, re], g_spec[a, rows, im]
                    pr, pi = p_spec[i - a, rows, re], p_spec[i - a, rows, im]
                    t_re, t_im = gr * pr - gi * pi, gr * pi + gi * pr
                    acc_re = t_re if acc_re is None else acc_re + t_re
                    acc_im = t_im if acc_im is None else acc_im + t_im
                for value, cols in ((acc_re, re), (acc_im, im)):
                    high = value.astype(BF16)
                    acc_high[i, rows, cols] = high
                    acc_low[i, rows, cols] = (value - high.astype(F32)).astype(BF16)
        return carry

    lax.fori_loop(0, ch // subs, products, 0)

    for b in range(0, blocks, group):
        high = acc_high[b : b + group].reshape(group * ch, 2 * n)
        low = acc_low[b : b + group].reshape(group * ch, 2 * n)
        conv = (inverse(high, 0) + inverse(low, 0) + inverse(high, 1)).reshape(group, ch, n)
        gated = packed[b : b + group, :ch, :].astype(F32)
        rows = (conv + skip[...][None] * gated).astype(BF16)
        out[b : b + group, :, :n] = rows
        other = (b + blocks // 2) % blocks
        out[other : other + group, :, n:] = rows[:, :, : n // 2]
    copies[2].wait()


def convolve(packed, skip, table, gate, gate_other, weight):
    blocks, both, n = packed.shape
    ch = both // 2
    near, far = pl.BlockSpec(memory_space=pltpu.VMEM), pl.BlockSpec(memory_space=pltpu.HBM)
    return pl.pallas_call(
        conv_kernel,
        in_specs=[near, near, near, far, far, far],
        out_specs=[near] * 3,
        out_shape=[
            jax.ShapeDtypeStruct((blocks, ch, n + n // 2), BF16),
            jax.ShapeDtypeStruct((gate.shape[1], n + n // 2), BF16),
            jax.ShapeDtypeStruct(weight.shape, BF16),
        ],
        scratch_shapes=[
            pltpu.VMEM(table.shape, BF16),
            pltpu.VMEM(gate.shape, BF16),
            pltpu.VMEM((blocks, ch, 2 * n), F32),
            pltpu.VMEM((blocks, ch, 2 * n), F32),
            pltpu.VMEM((blocks, ch, 2 * n), BF16),
            pltpu.VMEM((blocks, ch, 2 * n), BF16),
            pltpu.SemaphoreType.DMA((3,)),
        ],
        compiler_params=pltpu.CompilerParams(vmem_limit_bytes=28 * 2**20),
        name="convolve",
    )(packed, skip, gate_other, table, gate, weight)


def on_chip(body, shapes, *args, flops=0):
    in_vmem = pl.BlockSpec(memory_space=pltpu.VMEM)
    return pl.pallas_call(
        body,
        in_specs=[in_vmem] * len(args),
        out_specs=[in_vmem] * len(shapes),
        out_shape=[jax.ShapeDtypeStruct(shape, BF16) for shape in shapes],
        compiler_params=pltpu.CompilerParams(vmem_limit_bytes=8 * 2**20),
        cost_estimate=pl.CostEstimate(flops=flops, bytes_accessed=1, transcendentals=0),
    )(*args)


Z = 4


def project(weight, mixed, pieces, rows, chunk, split=False):
    channels, wide = mixed.shape
    tokens = wide // 3 * 2
    count = len(pieces)

    def body(weight, mixed, *outs):
        me = lax.axis_index("chan")
        for i, (flip, step, offset) in enumerate(pieces):
            start = ((me // Z + flip) % 2 * Z + (me % Z + step) % Z) * chunk + offset
            block = weight[pl.ds(pl.multiple_of(start, 16), rows), :]
            columns = mixed[:, wide - tokens :] if flip else mixed[:, :tokens]
            share = jnp.dot(block, columns, preferred_element_type=F32).astype(BF16)
            each = tokens // len(outs)
            for j, out in enumerate(outs):
                out[i] = share[:, j * each : (j + 1) * each]

    shapes = [(count, rows, tokens // 2)] * 2 if split else [(count, rows, tokens)]
    results = on_chip(body, shapes, weight, mixed, flops=2 * count * rows * channels * tokens)
    return results if split else results[0]


def to_z(block, step):
    n = lax.axis_size("chan")
    return lax.ppermute(block, "chan", [(i, i // Z * Z + (i + step) % Z) for i in range(n)])


def to_near_x(block):
    n = lax.axis_size("chan")
    return lax.ppermute(block, "chan", [(i, (i + Z) % n) for i in range(n)])


def to_far_x(block):
    n, m = lax.axis_size("chan"), lax.axis_size("seq")
    route = [(s * n + c, (s + m // 2) % m * n + (c + Z) % n) for s in range(m) for c in range(n)]
    return lax.ppermute(block, ("seq", "chan"), route)


def wide_sum(*terms):
    total = terms[0].astype(F32)
    for term in terms[1:]:
        total = total + term.astype(F32)
    return total


def beside(far, near):
    return jnp.concatenate([far.astype(F32), near.astype(F32)], axis=-1)


def shards(out_gate, in_gate, signal, filter_taps, skip_gain, out_proj):
    tokens, channels = out_gate.shape
    parts, chans = lax.axis_size("seq"), lax.axis_size("chan")
    per_part = channels // parts
    gate_other = lax.ppermute(out_gate[: tokens // 2], "seq", [(i, (i + parts // 2) % parts) for i in range(parts)])
    packed = prepare(in_gate, signal, filter_taps, parts)
    packed = lax.all_to_all(packed, "seq", 0, 0)
    skip = lax.dynamic_slice_in_dim(skip_gain, lax.axis_index("seq") * per_part, per_part, 0)
    table = jnp.asarray(transform_table(tokens))
    conv, out_gate_t, out_proj = convolve(packed, skip[:, None], table, out_gate, gate_other, out_proj)
    conv = lax.all_to_all(conv, "seq", 0, 0).reshape(channels, -1)
    mixed = (out_gate_t.astype(F32) * conv.astype(F32)).astype(BF16)

    chunk = out_proj.shape[0] // chans
    half_a = 320
    half_b = chunk // 2 - half_a
    order = [(2, 0), (1, 1), (2, 1), (3, 0), (1, 0), (3, 1), (0, 0), (0, 1)]
    rows_a = [[(flip, s, h * half_a) for s, h in order] for flip in (0, 1)]
    rows_b = [(flip, s, 2 * half_a + h * half_b) for s, h in order for flip in (0, 1)]
    half = tokens // 2

    near, far = project(out_proj, mixed, rows_a[1][:4], half_a, chunk, split=True)
    near_early, far_early = to_near_x(near), to_far_x(far)
    plus_b = project(out_proj, mixed, rows_b[:4], half_b, chunk)
    below_b = to_z(plus_b, 1)
    minus_b = project(out_proj, mixed, rows_b[4:8], half_b, chunk)
    above_b = to_z(minus_b, -1)
    near, far = project(out_proj, mixed, rows_a[1][4:], half_a, chunk, split=True)
    near_late, far_late = to_near_x(near), to_far_x(far)
    own_a = project(out_proj, mixed, rows_a[0], half_a, chunk)
    rest_b = project(out_proj, mixed, rows_b[8:], half_b, chunk)

    def first_a(own, near, far, plus, minus):
        total = wide_sum(own[:4], beside(far[...], near[...])).astype(BF16)
        plus[...] = total[:2]
        minus[...] = total[2:]

    plus_a, minus_a = on_chip(first_a, [(2, half_a, tokens)] * 2, own_a, near_early, far_early)
    below_a, above_a = to_z(plus_a, 1), to_z(minus_a, -1)

    def second_b(place):
        def body(rest, arrived, out):
            out[...] = wide_sum(rest[place : place + 2], arrived[:2]).astype(BF16)

        return body

    (up_b,) = on_chip(second_b(0), [(2, half_b, tokens)], rest_b, below_b)
    up_b = to_z(up_b, 1)
    (down_b,) = on_chip(second_b(2), [(2, half_b, tokens)], rest_b, above_b)
    down_b = to_z(down_b, -1)

    def second_a(place):
        def body(own, near, far, arrived, out):
            x_sum = beside(far[place : place + 1], near[place : place + 1])
            out[...] = wide_sum(own[4 + place : 5 + place], x_sum, arrived[:1]).astype(BF16)

        return body

    (up_a,) = on_chip(second_a(0), [(1, half_a, tokens)], own_a, near_late, far_late, below_a)
    up_a = to_z(up_a, 1)
    (down_a,) = on_chip(second_a(1), [(1, half_a, tokens)], own_a, near_late, far_late, above_a)
    down_a = to_z(down_a, -1)

    def reduced_b(flip, rest, below, above, up, down):
        first = wide_sum(rest[4 + flip], above[2 + flip], up[flip])
        second = wide_sum(rest[6 + flip], below[2 + flip], down[flip])
        return jnp.concatenate([first, second], axis=0)

    def third_b(rest, below, above, up, down, near, far):
        total = reduced_b(1, rest, below, above, up, down).astype(BF16)
        near[...] = total[:, :half]
        far[...] = total[:, half:]

    near_b, far_b = on_chip(third_b, [(2 * half_b, half)] * 2, rest_b, below_b, above_b, up_b, down_b)
    near_b, far_b = to_near_x(near_b), to_far_x(far_b)

    def last(own, near, far, below, above, up, down, rest, b_below, b_above, b_up, b_down, b_near, b_far, out, all_rows):
        first = wide_sum(own[6], beside(far[2], near[2]), above[1], up[0])
        second = wide_sum(own[7], beside(far[3], near[3]), below[1], down[0])
        all_rows[:half_a] = first.astype(BF16)
        all_rows[half_a : 2 * half_a] = second.astype(BF16)
        b_rows = reduced_b(0, rest, b_below, b_above, b_up, b_down) + beside(b_far[...], b_near[...])
        all_rows[2 * half_a :] = b_rows.astype(BF16)
        out[...] = all_rows[...].T

    out, _ = on_chip(
        last, [(tokens, chunk), (chunk, tokens)], own_a, near_late, far_late, below_a, above_a, up_a, down_a,
        rest_b, below_b, above_b, up_b, down_b, near_b, far_b,
    )
    return out


def solution(mesh):
    return jax.shard_map(
        shards,
        mesh=mesh,
        in_specs=(
            P("seq", "chan"),
            P("seq", "chan"),
            P("seq", "chan"),
            P("seq", "chan"),
            P("chan"),
            P(None, "chan"),
        ),
        out_specs=P("seq", "chan"),
        check_vma=False,
    )
```

```python
import numpy as np

import jax
import jax.numpy as jnp
from jax import lax
from jax.experimental import pallas as pl
from jax.experimental.pallas import tpu as pltpu
from jax.sharding import PartitionSpec as P

F32, BF16 = jnp.float32, jnp.bfloat16


def split_bf16(table):
    high = table.astype(BF16)
    low = (table - high.astype(np.float64)).astype(BF16)
    return high, low


def transform_table(n):
    freq = np.arange(n, dtype=np.float64) + 0.5
    angle = np.pi / n * np.outer(np.arange(n, dtype=np.float64), freq)
    forward = np.concatenate([np.cos(angle), -np.sin(angle)], axis=1)
    high, low = split_bf16(forward)
    inverse = [part.T.astype(np.float64) / n for part in (high, low)]
    return np.concatenate([high, low, np.concatenate(inverse, axis=1).astype(BF16)], axis=0)


def prepare_kernel(in_gate, signal, taps, packed, gate_buf, signal_buf, taps_buf, sems):
    parts, both, tokens = packed.shape
    half = both // 2
    steps, wide = gate_buf.shape[0], gate_buf.shape[2]
    copies = [
        [
            pltpu.make_async_copy(source.at[:, i * wide : (i + 1) * wide], buf.at[i], sems.at[i, j])
            for j, (source, buf) in enumerate(((in_gate, gate_buf), (signal, signal_buf), (taps, taps_buf)))
        ]
        for i in range(steps)
    ]
    for step in copies:
        for copy in step:
            copy.start()
    count = wide // half
    for i, step in enumerate(copies):
        for copy in step:
            copy.wait()
        gated = (gate_buf[i].astype(F32) * signal_buf[i].astype(F32)).astype(BF16)
        packed[i * count : (i + 1) * count, :half] = gated.T.reshape(count, half, tokens)
        packed[i * count : (i + 1) * count, half:] = taps_buf[i].T.reshape(count, half, tokens)


def prepare(in_gate, signal, taps, parts):
    tokens, channels = in_gate.shape
    steps = 4
    wide = channels // steps
    return pl.pallas_call(
        prepare_kernel,
        in_specs=[pl.BlockSpec(memory_space=pltpu.HBM)] * 3,
        out_specs=pl.BlockSpec(memory_space=pltpu.VMEM),
        out_shape=jax.ShapeDtypeStruct((parts, 2 * channels // parts, tokens), BF16),
        scratch_shapes=[pltpu.VMEM((steps, tokens, wide), BF16)] * 3 + [pltpu.SemaphoreType.DMA((steps, 3))],
        compiler_params=pltpu.CompilerParams(vmem_limit_bytes=60 * 2**20),
        name="prepare",
    )(in_gate, signal, taps)


def conv_kernel(
    packed, skip, table_far, weight_far, out, weight, table, g_spec, p_spec, acc_high, acc_low, sems
):
    copies = [
        pltpu.make_async_copy(source, target, sems.at[i])
        for i, (source, target) in enumerate(((table_far, table), (weight_far, weight)))
    ]
    for copy in copies:
        copy.start()
    copies[0].wait()
    blocks, both, n = packed.shape
    ch = both // 2
    lane = lax.broadcasted_iota(jnp.int32, (1, n), 1)
    sign = jnp.where(lane % 2 == 0, 1.0, -1.0).astype(F32)

    def transform(rows):
        return jnp.dot(rows, table[:n], preferred_element_type=F32) + jnp.dot(
            rows, table[n : 2 * n], preferred_element_type=F32
        )

    def inverse(spectra, part):
        return jnp.dot(spectra, table[2 * n :, part * n : (part + 1) * n], preferred_element_type=F32)

    group = 4
    tail = None
    for b in range(0, blocks, group):
        rows = packed[b : b + group]
        g_spec[b : b + group] = transform(rows[:, :ch].reshape(group * ch, n)).reshape(group, ch, 2 * n)
        h = transform(rows[:, ch:].reshape(group * ch, n)).reshape(group, ch, 2 * n)
        for j in range(group):
            if tail is None:
                p_spec[b + j] = h[j]
            else:
                p_spec[b + j, :, :n] = h[j, :, :n] - sign * tail[:, n:]
                p_spec[b + j, :, n:] = h[j, :, n:] + sign * tail[:, :n]
            tail = h[j]

    lanes, subs = 128, 16

    def products(step, carry):
        rows = pl.ds(pl.multiple_of(step * subs, subs), subs)
        for f in range(0, n, lanes):
            re, im = slice(f, f + lanes), slice(n + f, n + f + lanes)
            for i in range(blocks):
                acc_re = acc_im = None
                for a in range(i + 1):
                    gr, gi = g_spec[a, rows, re], g_spec[a, rows, im]
                    pr, pi = p_spec[i - a, rows, re], p_spec[i - a, rows, im]
                    t_re, t_im = gr * pr - gi * pi, gr * pi + gi * pr
                    acc_re = t_re if acc_re is None else acc_re + t_re
                    acc_im = t_im if acc_im is None else acc_im + t_im
                for value, cols in ((acc_re, re), (acc_im, im)):
                    high = value.astype(BF16)
                    acc_high[i, rows, cols] = high
                    acc_low[i, rows, cols] = (value - high.astype(F32)).astype(BF16)
        return carry

    lax.fori_loop(0, ch // subs, products, 0)

    for b in range(0, blocks, group):
        high = acc_high[b : b + group].reshape(group * ch, 2 * n)
        low = acc_low[b : b + group].reshape(group * ch, 2 * n)
        conv = (inverse(high, 0) + inverse(low, 0) + inverse(high, 1)).reshape(group, ch, n)
        gated = packed[b : b + group, :ch, :].astype(F32)
        out[b : b + group] = (conv + skip[...][None] * gated).astype(BF16)
    copies[1].wait()


def convolve(packed, skip, table, weight):
    blocks, both, n = packed.shape
    ch = both // 2
    near, far = pl.BlockSpec(memory_space=pltpu.VMEM), pl.BlockSpec(memory_space=pltpu.HBM)
    return pl.pallas_call(
        conv_kernel,
        in_specs=[near, near, far, far],
        out_specs=[near] * 2,
        out_shape=[
            jax.ShapeDtypeStruct((blocks, ch, n), BF16),
            jax.ShapeDtypeStruct(weight.shape, BF16),
        ],
        scratch_shapes=[
            pltpu.VMEM(table.shape, BF16),
            pltpu.VMEM((blocks, ch, 2 * n), F32),
            pltpu.VMEM((blocks, ch, 2 * n), F32),
            pltpu.VMEM((blocks, ch, 2 * n), BF16),
            pltpu.VMEM((blocks, ch, 2 * n), BF16),
            pltpu.SemaphoreType.DMA((2,)),
        ],
        compiler_params=pltpu.CompilerParams(vmem_limit_bytes=28 * 2**20),
        name="convolve",
    )(packed, skip, table, weight)


def on_chip(body, shapes, *args, flops=0):
    in_vmem = pl.BlockSpec(memory_space=pltpu.VMEM)
    return pl.pallas_call(
        body,
        in_specs=[in_vmem] * len(args),
        out_specs=[in_vmem] * len(shapes),
        out_shape=[jax.ShapeDtypeStruct(shape, BF16) for shape in shapes],
        compiler_params=pltpu.CompilerParams(vmem_limit_bytes=8 * 2**20),
        cost_estimate=pl.CostEstimate(flops=flops, bytes_accessed=1, transcendentals=0),
    )(*args)


Z = 4


def project(weight, mixed, groups, rows, chunk):
    channels, tokens = mixed.shape

    def body(weight, mixed, *outs):
        me = lax.axis_index("chan")
        for pieces, out in zip(groups, outs, strict=True):
            for i, (flip, step, offset) in enumerate(pieces):
                start = ((me // Z + flip) % 2 * Z + (me % Z + step) % Z) * chunk + offset
                block = weight[pl.ds(pl.multiple_of(start, 16), rows), :]
                out[i] = jnp.dot(block, mixed[...], preferred_element_type=F32).astype(BF16)

    shapes = [(len(pieces), rows, tokens) for pieces in groups]
    total = sum(shape[0] for shape in shapes) * rows
    return on_chip(body, shapes, weight, mixed, flops=2 * total * channels * tokens)


def to_z(block, step):
    n = lax.axis_size("chan")
    return lax.ppermute(block, "chan", [(i, i // Z * Z + (i + step) % Z) for i in range(n)])


def to_x(block):
    n = lax.axis_size("chan")
    return lax.ppermute(block, "chan", [(i, (i + Z) % n) for i in range(n)])


def wide_sum(*terms):
    total = terms[0].astype(F32)
    for term in terms[1:]:
        total = total + term.astype(F32)
    return total


def add(*parts):
    arrays = [part[0] for part in parts]
    cuts = [part[1:] for part in parts]

    def body(*refs):
        refs[-1][...] = wide_sum(*(ref[a:b] for ref, (a, b) in zip(refs[:-1], cuts, strict=True))).astype(BF16)

    count = cuts[0][1] - cuts[0][0]
    (total,) = on_chip(body, [(count,) + arrays[0].shape[1:]], *arrays)
    return total


def shards(out_gate, in_gate, signal, filter_taps, skip_gain, out_proj):
    tokens, channels = out_gate.shape
    parts, chans = lax.axis_size("seq"), lax.axis_size("chan")
    per_part = channels // parts
    packed, out_gate = lax.optimization_barrier((prepare(in_gate, signal, filter_taps, parts), out_gate))

    def turn(gate, out):
        out[...] = gate[...].T

    (gate_t,) = on_chip(turn, [(channels, tokens)], out_gate)
    packed, gate_t = lax.optimization_barrier((lax.all_to_all(packed, "seq", 0, 0), gate_t))
    skip = lax.dynamic_slice_in_dim(skip_gain, lax.axis_index("seq") * per_part, per_part, 0)
    table = jnp.asarray(transform_table(tokens))
    conv, out_proj = convolve(packed, skip[:, None], table, out_proj)
    conv = lax.all_to_all(conv, "seq", 0, 0).reshape(channels, tokens)
    mixed = (gate_t.astype(F32) * conv.astype(F32)).astype(BF16)

    chunk = out_proj.shape[0] // chans
    half_a = 224
    half_b = chunk // 2 - half_a

    def rows_a(flip, *places):
        return [(flip, step, h * half_a) for step, h in places]

    def rows_b(*places):
        return [(flip, step, 2 * half_a + h * half_b) for step, h in places for flip in (0, 1)]

    early, late = ((2, 0), (1, 1), (2, 1), (3, 0)), ((1, 0), (3, 1), (0, 0), (0, 1))
    run = lambda rows, *groups: project(out_proj, mixed, groups, rows, chunk)
    relay_up, relay_down = run(half_b, rows_b((2, 0)), rows_b((2, 1)))
    relay_up, relay_down, mixed = lax.optimization_barrier((relay_up, relay_down, mixed))
    relayed_up, relayed_down = to_z(relay_up, 1), to_z(relay_down, -1)
    (x_early,) = run(half_a, rows_a(1, *early))
    x_early = to_x(x_early)
    direct_up, direct_down = run(half_b, rows_b((1, 1)), rows_b((3, 0)))
    b_below, b_above = to_z(direct_up, 1), to_z(direct_down, -1)
    (x_late,) = run(half_a, rows_a(1, *late))
    x_late = to_x(x_late)
    (rest_b,) = run(half_b, rows_b(*late))
    (own_a,) = run(half_a, rows_a(0, *early, *late))

    b_up = to_z(add((rest_b, 0, 2), (relayed_up, 0, 2)), 1)
    b_down = to_z(add((rest_b, 2, 4), (relayed_down, 0, 2)), -1)

    def first_a(own, arrived, up, down):
        total = wide_sum(own[:4], arrived[...]).astype(BF16)
        up[...] = total[:2]
        down[...] = total[2:]

    up, down = on_chip(first_a, [(2, half_a, tokens)] * 2, own_a, x_early)
    a_below, a_above = to_z(up, 1), to_z(down, -1)
    a_up = to_z(add((own_a, 4, 5), (x_late, 0, 1), (a_below, 0, 1)), 1)
    a_down = to_z(add((own_a, 5, 6), (x_late, 1, 2), (a_above, 0, 1)), -1)

    def reduced_b(flip, rest, below, above, up, down):
        first = wide_sum(rest[4 + flip], above[flip], up[flip])
        second = wide_sum(rest[6 + flip], below[flip], down[flip])
        return jnp.concatenate([first, second], axis=0)

    def third_b(*refs):
        refs[-1][...] = reduced_b(1, *refs[:-1]).astype(BF16)

    (x_last,) = on_chip(third_b, [(2 * half_b, tokens)], rest_b, b_below, b_above, b_up, b_down)
    x_last = to_x(x_last)

    def last(own, x_late, below, above, up, down, x_last, rest, b_below, b_above, b_up, b_down, out, all_rows):
        first = wide_sum(own[6], x_late[2], above[1], up[0])
        second = wide_sum(own[7], x_late[3], below[1], down[0])
        all_rows[:half_a] = first.astype(BF16)
        all_rows[half_a : 2 * half_a] = second.astype(BF16)
        b_rows = reduced_b(0, rest, b_below, b_above, b_up, b_down) + x_last[...].astype(F32)
        all_rows[2 * half_a :] = b_rows.astype(BF16)
        out[...] = all_rows[...].T

    out, _ = on_chip(
        last, [(tokens, chunk), (chunk, tokens)], own_a, x_late, a_below, a_above, a_up, a_down,
        x_last, rest_b, b_below, b_above, b_up, b_down,
    )
    return out


def solution(mesh):
    return jax.shard_map(
        shards,
        mesh=mesh,
        in_specs=(
            P("seq", "chan"),
            P("seq", "chan"),
            P("seq", "chan"),
            P("seq", "chan"),
            P("chan"),
            P(None, "chan"),
        ),
        out_specs=P("seq", "chan"),
        check_vma=False,
    )
```

```python
import functools

import numpy as np

import jax
import jax.numpy as jnp
from jax import lax
from jax.experimental import pallas as pl
from jax.experimental.pallas import tpu as pltpu
from jax.sharding import PartitionSpec as P

F32, BF16 = jnp.float32, jnp.bfloat16


def split_bf16(table):
    high = table.astype(BF16)
    low = (table - high.astype(np.float64)).astype(BF16)
    return high, low


def transform_table(n):
    freq = np.arange(n, dtype=np.float64) + 0.5
    angle = np.pi / n * np.outer(np.arange(n, dtype=np.float64), freq)
    forward = np.concatenate([np.cos(angle), -np.sin(angle)], axis=1)
    high, low = split_bf16(forward)
    inverse = [part.T.astype(np.float64) / n for part in (high, low)]
    return np.concatenate([high, low, np.concatenate(inverse, axis=1).astype(BF16)], axis=0)


def prepare_kernel(in_gate, signal, taps, packed, gate_buf, signal_buf, taps_buf, packed_buf, sems, out_sems):
    parts, both, tokens = packed.shape
    half = both // 2
    steps, wide = gate_buf.shape[0], gate_buf.shape[2]
    count = wide // half
    copies = [
        [
            pltpu.make_async_copy(source.at[:, i * wide : (i + 1) * wide], buf.at[i], sems.at[i, j])
            for j, (source, buf) in enumerate(((in_gate, gate_buf), (signal, signal_buf), (taps, taps_buf)))
        ]
        for i in range(steps)
    ]
    for step in copies:
        for copy in step:
            copy.start()
    results = []
    for i, step in enumerate(copies):
        for copy in step:
            copy.wait()
        gated = (gate_buf[i].astype(F32) * signal_buf[i].astype(F32)).astype(BF16)
        places = slice(i * count, (i + 1) * count)
        packed_buf[places, :half] = gated.T.reshape(count, half, tokens)
        packed_buf[places, half:] = taps_buf[i].T.reshape(count, half, tokens)
        results.append(pltpu.make_async_copy(packed_buf.at[places], packed.at[places], out_sems.at[i]))
        results[-1].start()
    for copy in results:
        copy.wait()


def prepare(in_gate, signal, taps, parts):
    tokens, channels = in_gate.shape
    steps = 4
    wide = channels // steps
    packed = jax.ShapeDtypeStruct((parts, 2 * channels // parts, tokens), BF16)
    return pl.pallas_call(
        prepare_kernel,
        in_specs=[pl.BlockSpec(memory_space=pltpu.HBM)] * 3,
        out_specs=pl.BlockSpec(memory_space=pltpu.HBM),
        out_shape=packed,
        scratch_shapes=[pltpu.VMEM((steps, tokens, wide), BF16)] * 3
        + [pltpu.VMEM(packed.shape, BF16), pltpu.SemaphoreType.DMA((steps, 3)), pltpu.SemaphoreType.DMA((steps,))],
        compiler_params=pltpu.CompilerParams(vmem_limit_bytes=60 * 2**20),
        name="prepare",
    )(in_gate, signal, taps)


TILE = 16
REACH = 4
LANES = 128


def conv_kernel(packed, skip, table, out, *scratch):
    g_specs, p_specs, highs, lows = scratch[:2], scratch[2:4], scratch[4:6], scratch[6:8]
    blocks, both, n = packed.shape
    ch = both // 2
    tiles, rows = ch // TILE, blocks * TILE
    real, imag = slice(0, n), slice(n, 2 * n)
    lane = lax.broadcasted_iota(jnp.int32, (1, n), 1)
    sign = jnp.where(lane % 2 == 0, 1.0, -1.0).astype(F32)

    def spectrum(first, columns):
        samples = packed[:, first : first + TILE, :].reshape(rows, n)
        high = jnp.dot(samples, table[:n, columns], preferred_element_type=F32)
        low = jnp.dot(samples, table[n : 2 * n, columns], preferred_element_type=F32)
        return (high + low).reshape(blocks, TILE, n)

    def spectra(tile):
        g_spec, p_spec = g_specs[tile % 2], p_specs[tile % 2]

        def gated(columns):
            def task():
                g_spec[:, :, columns] = spectrum(tile * TILE, columns)

            return task

        def pairs():
            re, im = (spectrum(ch + tile * TILE, columns) for columns in (real, imag))
            p_spec[0, :, real], p_spec[0, :, imag] = re[0], im[0]
            for k in range(1, blocks):
                p_spec[k, :, real] = re[k] - sign * im[k - 1]
                p_spec[k, :, imag] = im[k] + sign * re[k - 1]

        return [gated(real), gated(imag), pairs]

    def products(tile):
        g_spec, p_spec = g_specs[tile % 2], p_specs[tile % 2]
        high, low = highs[tile % 2], lows[tile % 2]

        def task(lanes, start):
            re, im = slice(lanes, lanes + LANES), slice(n + lanes, n + lanes + LANES)
            total, window = [None] * REACH, [None] * REACH
            for a in range(start + REACH):
                gr, gi = g_spec[a, :, re], g_spec[a, :, im]
                for r in reversed(range(REACH)):
                    lag = start + r - a
                    if lag < 0:
                        continue
                    fresh = a == 0 or r == 0
                    window[r] = (p_spec[lag, :, re], p_spec[lag, :, im]) if fresh else window[r - 1]
                    pr, pi = window[r]
                    term = (gr * pr - gi * pi, gr * pi + gi * pr)
                    total[r] = term if a == 0 else (total[r][0] + term[0], total[r][1] + term[1])
            for r in range(REACH):
                for value, columns in zip(total[r], (re, im), strict=True):
                    rounded = value.astype(BF16)
                    high[start + r, :, columns] = rounded
                    low[start + r, :, columns] = (value - rounded.astype(F32)).astype(BF16)

        return [
            functools.partial(task, lanes, start)
            for lanes in range(0, n, LANES)
            for start in range(0, blocks, REACH)
        ]

    def inverse(tile):
        def task():
            high = highs[tile % 2][...].reshape(rows, 2 * n)
            low = lows[tile % 2][...].reshape(rows, 2 * n)
            back, back_low = table[2 * n :, :n], table[2 * n :, n:]
            conv = (
                jnp.dot(high, back, preferred_element_type=F32)
                + jnp.dot(low, back, preferred_element_type=F32)
                + jnp.dot(high, back_low, preferred_element_type=F32)
            ).reshape(blocks, TILE, n)
            channels = slice(tile * TILE, (tile + 1) * TILE)
            gated = packed[:, channels, :].astype(F32)
            out[:, channels, :] = (conv + skip[channels][None] * gated).astype(BF16)

        return [task]

    for step in range(tiles + 2):
        matrix = inverse(step - 2) if step >= 2 else []
        matrix += spectra(step) if step < tiles else []
        vector = products(step - 1) if 0 <= step - 1 < tiles else []
        share = max(1, len(vector) // max(1, len(matrix)))
        while matrix or vector:
            for task in matrix[:1] + vector[:share]:
                task()
            matrix, vector = matrix[1:], vector[share:]


def convolve(packed, skip, table):
    blocks, both, n = packed.shape
    ch = both // 2
    near = pl.BlockSpec(memory_space=pltpu.VMEM)
    return pl.pallas_call(
        conv_kernel,
        in_specs=[near] * 3,
        out_specs=near,
        out_shape=jax.ShapeDtypeStruct((blocks, ch, n), BF16),
        scratch_shapes=[pltpu.VMEM((blocks, TILE, 2 * n), F32)] * 4 + [pltpu.VMEM((blocks, TILE, 2 * n), BF16)] * 4,
        compiler_params=pltpu.CompilerParams(vmem_limit_bytes=8 * 2**20),
        cost_estimate=pl.CostEstimate(flops=5 * 10**9, bytes_accessed=1, transcendentals=0),
        name="convolve",
    )(packed, skip, table)


def on_chip(body, shapes, *args, flops=0):
    in_vmem = pl.BlockSpec(memory_space=pltpu.VMEM)
    return pl.pallas_call(
        body,
        in_specs=[in_vmem] * len(args),
        out_specs=[in_vmem] * len(shapes),
        out_shape=[jax.ShapeDtypeStruct(shape, BF16) for shape in shapes],
        compiler_params=pltpu.CompilerParams(vmem_limit_bytes=8 * 2**20),
        cost_estimate=pl.CostEstimate(flops=flops, bytes_accessed=1, transcendentals=0),
    )(*args)


Z = 4


def project(weight, mixed, groups, rows, chunk):
    channels, tokens = mixed.shape

    def body(weight, mixed, *outs):
        me = lax.axis_index("chan")
        for pieces, out in zip(groups, outs, strict=True):
            for i, (flip, step, offset) in enumerate(pieces):
                start = ((me // Z + flip) % 2 * Z + (me % Z + step) % Z) * chunk + offset
                block = weight[pl.ds(pl.multiple_of(start, 16), rows), :]
                out[i] = jnp.dot(block, mixed[...], preferred_element_type=F32).astype(BF16)

    shapes = [(len(pieces), rows, tokens) for pieces in groups]
    total = sum(shape[0] for shape in shapes) * rows
    return on_chip(body, shapes, weight, mixed, flops=2 * total * channels * tokens)


def to_z(block, step):
    n = lax.axis_size("chan")
    return lax.ppermute(block, "chan", [(i, i // Z * Z + (i + step) % Z) for i in range(n)])


def to_x(block):
    n = lax.axis_size("chan")
    return lax.ppermute(block, "chan", [(i, (i + Z) % n) for i in range(n)])


def wide_sum(*terms):
    total = terms[0].astype(F32)
    for term in terms[1:]:
        total = total + term.astype(F32)
    return total


def add(*parts):
    arrays = [part[0] for part in parts]
    cuts = [part[1:] for part in parts]

    def body(*refs):
        refs[-1][...] = wide_sum(*(ref[a:b] for ref, (a, b) in zip(refs[:-1], cuts, strict=True))).astype(BF16)

    count = cuts[0][1] - cuts[0][0]
    (total,) = on_chip(body, [(count,) + arrays[0].shape[1:]], *arrays)
    return total


def shards(out_gate, in_gate, signal, filter_taps, skip_gain, out_proj):
    tokens, channels = out_gate.shape
    parts, chans = lax.axis_size("seq"), lax.axis_size("chan")
    per_part = channels // parts
    packed, out_gate = lax.optimization_barrier((prepare(in_gate, signal, filter_taps, parts), out_gate))

    def stage(gate, table, gate_t, staged):
        gate_t[...] = gate[...].T
        staged[...] = table[...]

    table = jnp.asarray(transform_table(tokens))
    gate_t, table = on_chip(stage, [(channels, tokens), table.shape], out_gate, table)
    packed, gate_t, table = lax.optimization_barrier((lax.all_to_all(packed, "seq", 0, 0), gate_t, table))
    skip = lax.dynamic_slice_in_dim(skip_gain, lax.axis_index("seq") * per_part, per_part, 0)
    conv = convolve(packed, skip[:, None], table)
    conv = lax.all_to_all(conv, "seq", 0, 0).reshape(channels, tokens)
    mixed = (gate_t.astype(F32) * conv.astype(F32)).astype(BF16)

    chunk = out_proj.shape[0] // chans
    half_a = 224
    half_b = chunk // 2 - half_a

    def rows_a(flip, *places):
        return [(flip, step, h * half_a) for step, h in places]

    def rows_b(*places):
        return [(flip, step, 2 * half_a + h * half_b) for step, h in places for flip in (0, 1)]

    early, late = ((2, 0), (1, 1), (2, 1), (3, 0)), ((1, 0), (3, 1), (0, 0), (0, 1))
    def run(rows, *groups):
        return project(out_proj, mixed, groups, rows, chunk)

    relay_up, relay_down = run(half_b, rows_b((2, 0)), rows_b((2, 1)))
    relay_up, relay_down, mixed = lax.optimization_barrier((relay_up, relay_down, mixed))
    relayed_up, relayed_down = to_z(relay_up, 1), to_z(relay_down, -1)
    (x_early,) = run(half_a, rows_a(1, *early))
    x_early, mixed = lax.optimization_barrier((x_early, mixed))
    x_early = to_x(x_early)
    direct_up, direct_down = run(half_b, rows_b((1, 1)), rows_b((3, 0)))
    b_below, b_above = to_z(direct_up, 1), to_z(direct_down, -1)
    (x_late,) = run(half_a, rows_a(1, *late))
    x_late = to_x(x_late)
    (rest_b,) = run(half_b, rows_b(*late))
    (own_a,) = run(half_a, rows_a(0, *early, *late))

    b_up = to_z(add((rest_b, 0, 2), (relayed_up, 0, 2)), 1)
    b_down = to_z(add((rest_b, 2, 4), (relayed_down, 0, 2)), -1)

    def first_a(own, arrived, up, down):
        total = wide_sum(own[:4], arrived[...]).astype(BF16)
        up[...] = total[:2]
        down[...] = total[2:]

    up, down = on_chip(first_a, [(2, half_a, tokens)] * 2, own_a, x_early)
    a_below, a_above = to_z(up, 1), to_z(down, -1)
    a_up = to_z(add((own_a, 4, 5), (x_late, 0, 1), (a_below, 0, 1)), 1)
    a_down = to_z(add((own_a, 5, 6), (x_late, 1, 2), (a_above, 0, 1)), -1)

    def reduced_b(flip, rest, below, above, up, down):
        first = wide_sum(rest[4 + flip], above[flip], up[flip])
        second = wide_sum(rest[6 + flip], below[flip], down[flip])
        return jnp.concatenate([first, second], axis=0)

    def third_b(*refs):
        refs[-1][...] = reduced_b(1, *refs[:-1]).astype(BF16)

    (x_last,) = on_chip(third_b, [(2 * half_b, tokens)], rest_b, b_below, b_above, b_up, b_down)
    x_last = to_x(x_last)

    def last(own, x_late, below, above, up, down, x_last, rest, b_below, b_above, b_up, b_down, out, all_rows):
        first = wide_sum(own[6], x_late[2], above[1], up[0])
        second = wide_sum(own[7], x_late[3], below[1], down[0])
        all_rows[:half_a] = first.astype(BF16)
        all_rows[half_a : 2 * half_a] = second.astype(BF16)
        b_rows = reduced_b(0, rest, b_below, b_above, b_up, b_down) + x_last[...].astype(F32)
        all_rows[2 * half_a :] = b_rows.astype(BF16)
        out[...] = all_rows[...].T

    out, _ = on_chip(
        last, [(tokens, chunk), (chunk, tokens)], own_a, x_late, a_below, a_above, a_up, a_down,
        x_last, rest_b, b_below, b_above, b_up, b_down,
    )
    return out


def solution(mesh):
    return jax.shard_map(
        shards,
        mesh=mesh,
        in_specs=(
            P("seq", "chan"),
            P("seq", "chan"),
            P("seq", "chan"),
            P("seq", "chan"),
            P("chan"),
            P(None, "chan"),
        ),
        out_specs=P("seq", "chan"),
        check_vma=False,
    )
```

```python
import functools

import numpy as np

import jax
import jax.numpy as jnp
from jax import lax
from jax.experimental import pallas as pl
from jax.experimental.pallas import tpu as pltpu
from jax.sharding import PartitionSpec as P

F32, BF16 = jnp.float32, jnp.bfloat16


def split_bf16(table):
    high = table.astype(BF16)
    low = (table - high.astype(np.float64)).astype(BF16)
    return high, low


def transform_table(n):
    freq = np.arange(n, dtype=np.float64) + 0.5
    angle = np.pi / n * np.outer(np.arange(n, dtype=np.float64), freq)
    forward = np.concatenate([np.cos(angle), -np.sin(angle)], axis=1)
    high, low = split_bf16(forward)
    inverse = [part.T.astype(np.float64) / n for part in (high, low)]
    return np.concatenate([high, low, np.concatenate(inverse, axis=1).astype(BF16)], axis=0)


def prepare_kernel(in_gate, signal, taps, packed, gate_buf, signal_buf, taps_buf, packed_buf, sems, out_sems):
    parts, both, tokens = packed.shape
    half = both // 2
    steps, wide = gate_buf.shape[0], gate_buf.shape[2]
    count = wide // half
    copies = [
        [
            pltpu.make_async_copy(source.at[:, i * wide : (i + 1) * wide], buf.at[i], sems.at[i, j])
            for j, (source, buf) in enumerate(((in_gate, gate_buf), (signal, signal_buf), (taps, taps_buf)))
        ]
        for i in range(steps)
    ]
    for step in copies:
        for copy in step:
            copy.start()
    results = []
    for i, step in enumerate(copies):
        for copy in step:
            copy.wait()
        gated = (gate_buf[i].astype(F32) * signal_buf[i].astype(F32)).astype(BF16)
        places = slice(i * count, (i + 1) * count)
        packed_buf[places, :half] = gated.T.reshape(count, half, tokens)
        packed_buf[places, half:] = taps_buf[i].T.reshape(count, half, tokens)
        results.append(pltpu.make_async_copy(packed_buf.at[places], packed.at[places], out_sems.at[i]))
        results[-1].start()
    for copy in results:
        copy.wait()


def prepare(in_gate, signal, taps, parts):
    tokens, channels = in_gate.shape
    steps = 4
    wide = channels // steps
    packed = jax.ShapeDtypeStruct((parts, 2 * channels // parts, tokens), BF16)
    return pl.pallas_call(
        prepare_kernel,
        in_specs=[pl.BlockSpec(memory_space=pltpu.HBM)] * 3,
        out_specs=pl.BlockSpec(memory_space=pltpu.HBM),
        out_shape=packed,
        scratch_shapes=[pltpu.VMEM((steps, tokens, wide), BF16)] * 3
        + [pltpu.VMEM(packed.shape, BF16), pltpu.SemaphoreType.DMA((steps, 3)), pltpu.SemaphoreType.DMA((steps,))],
        compiler_params=pltpu.CompilerParams(vmem_limit_bytes=60 * 2**20),
        name="prepare",
    )(in_gate, signal, taps)


TILE = 16
REACH = 4
LANES = 128


def conv_kernel(packed, skip, table, out, *scratch):
    g_specs, p_specs, highs, lows = scratch[:2], scratch[2:4], scratch[4:6], scratch[6:8]
    blocks, both, n = packed.shape
    ch = both // 2
    tiles, rows = ch // TILE, blocks * TILE
    real, imag, third = slice(0, n), slice(n, 2 * n), slice(2 * n, 3 * n)
    lane = lax.broadcasted_iota(jnp.int32, (1, n), 1)
    sign = jnp.where(lane % 2 == 0, 1.0, -1.0).astype(F32)

    def spectrum(first, columns):
        samples = packed[:, first : first + TILE, :].reshape(rows, n)
        high = jnp.dot(samples, table[:n, columns], preferred_element_type=F32)
        low = jnp.dot(samples, table[n : 2 * n, columns], preferred_element_type=F32)
        return (high + low).reshape(blocks, TILE, n)

    def spectra(tile):
        g_spec, p_spec = g_specs[tile % 2], p_specs[tile % 2]

        def gated():
            re, im = (spectrum(tile * TILE, columns) for columns in (real, imag))
            g_spec[:, :, real], g_spec[:, :, imag], g_spec[:, :, third] = re, im, re + im

        def pairs():
            re, im = (spectrum(ch + tile * TILE, columns) for columns in (real, imag))
            for k in range(blocks):
                pr, pi = (re[k] - sign * im[k - 1], im[k] + sign * re[k - 1]) if k else (re[k], im[k])
                p_spec[k, :, real], p_spec[k, :, imag], p_spec[k, :, third] = pr, pi - pr, pr + pi

        return [gated, pairs]

    def products(tile):
        g_spec, p_spec = g_specs[tile % 2], p_specs[tile % 2]
        high, low = highs[tile % 2], lows[tile % 2]

        def task(lanes, start):
            re, im, both = (slice(k * n + lanes, k * n + lanes + LANES) for k in range(3))
            total, window = [None] * REACH, [None] * REACH
            for a in range(start + REACH):
                gr, gi, gs = (g_spec[a, :, part] for part in (re, im, both))
                for r in reversed(range(REACH)):
                    lag = start + r - a
                    if lag < 0:
                        continue
                    fresh = a == 0 or r == 0
                    window[r] = tuple(p_spec[lag, :, part] for part in (re, im, both)) if fresh else window[r - 1]
                    pr, pd, ps = window[r]
                    term = (gs * pr, gr * pd, gi * ps)
                    total[r] = term if a == 0 else tuple(t + u for t, u in zip(total[r], term, strict=True))
            total = [(first - last, first + middle) for first, middle, last in total]
            for r in range(REACH):
                for value, columns in zip(total[r], (re, im), strict=True):
                    rounded = value.astype(BF16)
                    high[start + r, :, columns] = rounded
                    low[start + r, :, columns] = (value - rounded.astype(F32)).astype(BF16)

        return [
            functools.partial(task, lanes, start)
            for lanes in range(0, n, LANES)
            for start in range(0, blocks, REACH)
        ]

    def inverse(tile):
        def task():
            high = highs[tile % 2][...].reshape(rows, 2 * n)
            low = lows[tile % 2][...].reshape(rows, 2 * n)
            back, back_low = table[2 * n :, :n], table[2 * n :, n:]
            conv = (
                jnp.dot(high, back, preferred_element_type=F32)
                + jnp.dot(low, back, preferred_element_type=F32)
                + jnp.dot(high, back_low, preferred_element_type=F32)
            ).reshape(blocks, TILE, n)
            channels = slice(tile * TILE, (tile + 1) * TILE)
            gated = packed[:, channels, :].astype(F32)
            out[:, channels, :] = (conv + skip[channels][None] * gated).astype(BF16)

        return [task]

    for step in range(tiles + 2):
        matrix = inverse(step - 2) if step >= 2 else []
        matrix += spectra(step) if step < tiles else []
        vector = products(step - 1) if 0 <= step - 1 < tiles else []
        share = max(1, len(vector) // max(1, len(matrix)))
        while matrix or vector:
            for task in matrix[:1] + vector[:share]:
                task()
            matrix, vector = matrix[1:], vector[share:]


def convolve(packed, skip, table):
    blocks, both, n = packed.shape
    ch = both // 2
    near = pl.BlockSpec(memory_space=pltpu.VMEM)
    return pl.pallas_call(
        conv_kernel,
        in_specs=[near] * 3,
        out_specs=near,
        out_shape=jax.ShapeDtypeStruct((blocks, ch, n), BF16),
        scratch_shapes=[pltpu.VMEM((blocks, TILE, 3 * n), F32)] * 4 + [pltpu.VMEM((blocks, TILE, 2 * n), BF16)] * 4,
        compiler_params=pltpu.CompilerParams(vmem_limit_bytes=10 * 2**20),
        cost_estimate=pl.CostEstimate(flops=5 * 10**9, bytes_accessed=1, transcendentals=0),
        name="convolve",
    )(packed, skip, table)


def on_chip(body, shapes, *args, flops=0):
    in_vmem = pl.BlockSpec(memory_space=pltpu.VMEM)
    return pl.pallas_call(
        body,
        in_specs=[in_vmem] * len(args),
        out_specs=[in_vmem] * len(shapes),
        out_shape=[jax.ShapeDtypeStruct(shape, BF16) for shape in shapes],
        compiler_params=pltpu.CompilerParams(vmem_limit_bytes=8 * 2**20),
        cost_estimate=pl.CostEstimate(flops=flops, bytes_accessed=1, transcendentals=0),
    )(*args)


Z = 4


def project(weight, mixed, groups, rows, chunk):
    channels, tokens = mixed.shape

    def body(weight, mixed, *outs):
        me = lax.axis_index("chan")
        for pieces, out in zip(groups, outs, strict=True):
            for i, (flip, step, offset) in enumerate(pieces):
                start = ((me // Z + flip) % 2 * Z + (me % Z + step) % Z) * chunk + offset
                block = weight[pl.ds(pl.multiple_of(start, 16), rows), :]
                out[i] = jnp.dot(block, mixed[...], preferred_element_type=F32).astype(BF16)

    shapes = [(len(pieces), rows, tokens) for pieces in groups]
    total = sum(shape[0] for shape in shapes) * rows
    return on_chip(body, shapes, weight, mixed, flops=2 * total * channels * tokens)


def to_z(block, step):
    n = lax.axis_size("chan")
    return lax.ppermute(block, "chan", [(i, i // Z * Z + (i + step) % Z) for i in range(n)])


def to_x(block):
    n = lax.axis_size("chan")
    return lax.ppermute(block, "chan", [(i, (i + Z) % n) for i in range(n)])


def wide_sum(*terms):
    total = terms[0].astype(F32)
    for term in terms[1:]:
        total = total + term.astype(F32)
    return total


def add(*parts):
    arrays = [part[0] for part in parts]
    cuts = [part[1:] for part in parts]

    def body(*refs):
        refs[-1][...] = wide_sum(*(ref[a:b] for ref, (a, b) in zip(refs[:-1], cuts, strict=True))).astype(BF16)

    count = cuts[0][1] - cuts[0][0]
    (total,) = on_chip(body, [(count,) + arrays[0].shape[1:]], *arrays)
    return total


def shards(out_gate, in_gate, signal, filter_taps, skip_gain, out_proj):
    tokens, channels = out_gate.shape
    parts, chans = lax.axis_size("seq"), lax.axis_size("chan")
    per_part = channels // parts
    packed, out_gate = lax.optimization_barrier((prepare(in_gate, signal, filter_taps, parts), out_gate))

    def stage(gate, table, gate_t, staged):
        gate_t[...] = gate[...].T
        staged[...] = table[...]

    table = jnp.asarray(transform_table(tokens))
    gate_t, table = on_chip(stage, [(channels, tokens), table.shape], out_gate, table)
    packed, gate_t, table = lax.optimization_barrier((lax.all_to_all(packed, "seq", 0, 0), gate_t, table))
    skip = lax.dynamic_slice_in_dim(skip_gain, lax.axis_index("seq") * per_part, per_part, 0)
    conv = convolve(packed, skip[:, None], table)
    conv = lax.all_to_all(conv, "seq", 0, 0).reshape(channels, tokens)
    mixed = (gate_t.astype(F32) * conv.astype(F32)).astype(BF16)

    chunk = out_proj.shape[0] // chans
    half_a = 240
    half_b = chunk // 2 - half_a

    def rows_a(flip, *places):
        return [(flip, step, h * half_a) for step, h in places]

    def rows_b(*places):
        return [(flip, step, 2 * half_a + h * half_b) for step, h in places for flip in (0, 1)]

    early, late = ((2, 0), (1, 1), (2, 1), (3, 0)), ((1, 0), (3, 1), (0, 0), (0, 1))
    def run(rows, *groups):
        return project(out_proj, mixed, groups, rows, chunk)

    relay_up, relay_down = run(half_b, rows_b((2, 0)), rows_b((2, 1)))
    relay_up, relay_down, mixed = lax.optimization_barrier((relay_up, relay_down, mixed))
    relayed_up, relayed_down = to_z(relay_up, 1), to_z(relay_down, -1)
    (x_early,) = run(half_a, rows_a(1, *early))
    x_early, mixed = lax.optimization_barrier((x_early, mixed))
    x_early = to_x(x_early)
    direct_up, direct_down = run(half_b, rows_b((1, 1)), rows_b((3, 0)))
    b_below, b_above = to_z(direct_up, 1), to_z(direct_down, -1)
    (rest_b,) = run(half_b, rows_b(*late))
    (x_late,) = run(half_a, rows_a(1, *late))
    (own_a,) = run(half_a, rows_a(0, *early, *late))
    rest_b, x_late, own_a = lax.optimization_barrier((rest_b, x_late, own_a))
    x_late = to_x(x_late)

    b_up = to_z(add((rest_b, 0, 2), (relayed_up, 0, 2)), 1)
    b_down = to_z(add((rest_b, 2, 4), (relayed_down, 0, 2)), -1)

    def first_a(own, arrived, up, down):
        total = wide_sum(own[:4], arrived[...]).astype(BF16)
        up[...] = total[:2]
        down[...] = total[2:]

    up, down = on_chip(first_a, [(2, half_a, tokens)] * 2, own_a, x_early)
    a_below, a_above = to_z(up, 1), to_z(down, -1)
    a_up = to_z(add((own_a, 4, 5), (x_late, 0, 1), (a_below, 0, 1)), 1)
    a_down = to_z(add((own_a, 5, 6), (x_late, 1, 2), (a_above, 0, 1)), -1)

    def reduced_b(flip, rest, below, above, up, down):
        first = wide_sum(rest[4 + flip], above[flip], up[flip])
        second = wide_sum(rest[6 + flip], below[flip], down[flip])
        return jnp.concatenate([first, second], axis=0)

    def third_b(*refs):
        refs[-1][...] = reduced_b(1, *refs[:-1]).astype(BF16)

    (x_last,) = on_chip(third_b, [(2 * half_b, tokens)], rest_b, b_below, b_above, b_up, b_down)
    x_last = to_x(x_last)

    def last(own, x_late, below, above, up, down, x_last, rest, b_below, b_above, b_up, b_down, out, all_rows):
        first = wide_sum(own[6], x_late[2], above[1], up[0])
        second = wide_sum(own[7], x_late[3], below[1], down[0])
        all_rows[:half_a] = first.astype(BF16)
        all_rows[half_a : 2 * half_a] = second.astype(BF16)
        b_rows = reduced_b(0, rest, b_below, b_above, b_up, b_down) + x_last[...].astype(F32)
        all_rows[2 * half_a :] = b_rows.astype(BF16)
        out[...] = all_rows[...].T

    out, _ = on_chip(
        last, [(tokens, chunk), (chunk, tokens)], own_a, x_late, a_below, a_above, a_up, a_down,
        x_last, rest_b, b_below, b_above, b_up, b_down,
    )
    return out


def solution(mesh):
    return jax.shard_map(
        shards,
        mesh=mesh,
        in_specs=(
            P("seq", "chan"),
            P("seq", "chan"),
            P("seq", "chan"),
            P("seq", "chan"),
            P("chan"),
            P(None, "chan"),
        ),
        out_specs=P("seq", "chan"),
        check_vma=False,
    )
```

```python
import functools

import numpy as np

import jax
import jax.numpy as jnp
from jax import lax
from jax.experimental import pallas as pl
from jax.experimental.pallas import tpu as pltpu
from jax.sharding import PartitionSpec as P

F32, BF16 = jnp.float32, jnp.bfloat16


def split_bf16(table):
    high = table.astype(BF16)
    low = (table - high.astype(np.float64)).astype(BF16)
    return high, low


def transform_table(n):
    freq = np.arange(n, dtype=np.float64) + 0.5
    angle = np.pi / n * np.outer(np.arange(n, dtype=np.float64), freq)
    forward = np.concatenate([np.cos(angle), -np.sin(angle)], axis=1)
    high, low = split_bf16(forward)
    inverse = [part.T.astype(np.float64) / n for part in (high, low)]
    return np.concatenate([high, low, np.concatenate(inverse, axis=1).astype(BF16)], axis=0)


def prepare_kernel(in_gate, signal, taps, packed, gate_buf, signal_buf, taps_buf, packed_buf, sems, out_sems):
    parts, both, tokens = packed.shape
    half = both // 2
    steps, wide = gate_buf.shape[0], gate_buf.shape[2]
    count = wide // half
    copies = [
        [
            pltpu.make_async_copy(source.at[:, i * wide : (i + 1) * wide], buf.at[i], sems.at[i, j])
            for j, (source, buf) in enumerate(((in_gate, gate_buf), (signal, signal_buf), (taps, taps_buf)))
        ]
        for i in range(steps)
    ]
    for step in copies:
        for copy in step:
            copy.start()
    results = []
    for i, step in enumerate(copies):
        for copy in step:
            copy.wait()
        gated = (gate_buf[i].astype(F32) * signal_buf[i].astype(F32)).astype(BF16)
        places = slice(i * count, (i + 1) * count)
        packed_buf[places, :half] = gated.T.reshape(count, half, tokens)
        packed_buf[places, half:] = taps_buf[i].T.reshape(count, half, tokens)
        results.append(pltpu.make_async_copy(packed_buf.at[places], packed.at[places], out_sems.at[i]))
        results[-1].start()
    for copy in results:
        copy.wait()


def prepare(in_gate, signal, taps, parts):
    tokens, channels = in_gate.shape
    steps = 4
    wide = channels // steps
    packed = jax.ShapeDtypeStruct((parts, 2 * channels // parts, tokens), BF16)
    return pl.pallas_call(
        prepare_kernel,
        in_specs=[pl.BlockSpec(memory_space=pltpu.HBM)] * 3,
        out_specs=pl.BlockSpec(memory_space=pltpu.HBM),
        out_shape=packed,
        scratch_shapes=[pltpu.VMEM((steps, tokens, wide), BF16)] * 3
        + [pltpu.VMEM(packed.shape, BF16), pltpu.SemaphoreType.DMA((steps, 3)), pltpu.SemaphoreType.DMA((steps,))],
        compiler_params=pltpu.CompilerParams(vmem_limit_bytes=60 * 2**20),
        name="prepare",
    )(in_gate, signal, taps)


TILE = 16
REACH = 4
LANES = 128


def conv_kernel(packed, skip, table, out, *scratch):
    g_specs, p_specs, highs, lows = scratch[:2], scratch[2:4], scratch[4:6], scratch[6:8]
    blocks, both, n = packed.shape
    ch = both // 2
    tiles, rows = ch // TILE, blocks * TILE
    real, imag, third = slice(0, n), slice(n, 2 * n), slice(2 * n, 3 * n)
    lane = lax.broadcasted_iota(jnp.int32, (1, n), 1)
    sign = jnp.where(lane % 2 == 0, 1.0, -1.0).astype(F32)

    def spectrum(first, columns):
        samples = packed[:, first : first + TILE, :].reshape(rows, n)
        high = jnp.dot(samples, table[:n, columns], preferred_element_type=F32)
        low = jnp.dot(samples, table[n : 2 * n, columns], preferred_element_type=F32)
        return (high + low).reshape(blocks, TILE, n)

    def spectra(tile):
        g_spec, p_spec = g_specs[tile % 2], p_specs[tile % 2]

        def gated():
            re, im = (spectrum(tile * TILE, columns) for columns in (real, imag))
            g_spec[:, :, real], g_spec[:, :, imag], g_spec[:, :, third] = re, im, re + im

        def pairs():
            re, im = (spectrum(ch + tile * TILE, columns) for columns in (real, imag))
            for k in range(blocks):
                pr, pi = (re[k] - sign * im[k - 1], im[k] + sign * re[k - 1]) if k else (re[k], im[k])
                p_spec[k, :, real], p_spec[k, :, imag], p_spec[k, :, third] = pr, pi - pr, pr + pi

        return [gated, pairs]

    def products(tile):
        g_spec, p_spec = g_specs[tile % 2], p_specs[tile % 2]
        high, low = highs[tile % 2], lows[tile % 2]

        def task(lanes, start):
            re, im, both = (slice(k * n + lanes, k * n + lanes + LANES) for k in range(3))
            total, window = [None] * REACH, [None] * REACH
            for a in range(start + REACH):
                gr, gi, gs = (g_spec[a, :, part] for part in (re, im, both))
                for r in reversed(range(REACH)):
                    lag = start + r - a
                    if lag < 0:
                        continue
                    fresh = a == 0 or r == 0
                    window[r] = tuple(p_spec[lag, :, part] for part in (re, im, both)) if fresh else window[r - 1]
                    pr, pd, ps = window[r]
                    term = (gs * pr, gr * pd, gi * ps)
                    total[r] = term if a == 0 else tuple(t + u for t, u in zip(total[r], term, strict=True))
            total = [(first - last, first + middle) for first, middle, last in total]
            for r in range(REACH):
                for value, columns in zip(total[r], (re, im), strict=True):
                    rounded = value.astype(BF16)
                    high[start + r, :, columns] = rounded
                    low[start + r, :, columns] = (value - rounded.astype(F32)).astype(BF16)

        return [
            functools.partial(task, lanes, start)
            for lanes in range(0, n, LANES)
            for start in range(0, blocks, REACH)
        ]

    def inverse(tile):
        def task():
            high = highs[tile % 2][...].reshape(rows, 2 * n)
            low = lows[tile % 2][...].reshape(rows, 2 * n)
            back, back_low = table[2 * n :, :n], table[2 * n :, n:]
            conv = (
                jnp.dot(high, back, preferred_element_type=F32)
                + jnp.dot(low, back, preferred_element_type=F32)
                + jnp.dot(high, back_low, preferred_element_type=F32)
            ).reshape(blocks, TILE, n)
            channels = slice(tile * TILE, (tile + 1) * TILE)
            gated = packed[:, channels, :].astype(F32)
            out[:, channels, :] = (conv + skip[channels][None] * gated).astype(BF16)

        return [task]

    for step in range(tiles + 2):
        matrix = inverse(step - 2) if step >= 2 else []
        matrix += spectra(step) if step < tiles else []
        vector = products(step - 1) if 0 <= step - 1 < tiles else []
        share = max(1, len(vector) // max(1, len(matrix)))
        while matrix or vector:
            for task in matrix[:1] + vector[:share]:
                task()
            matrix, vector = matrix[1:], vector[share:]


def convolve(packed, skip, table):
    blocks, both, n = packed.shape
    ch = both // 2
    near = pl.BlockSpec(memory_space=pltpu.VMEM)
    return pl.pallas_call(
        conv_kernel,
        in_specs=[near] * 3,
        out_specs=near,
        out_shape=jax.ShapeDtypeStruct((blocks, ch, n), BF16),
        scratch_shapes=[pltpu.VMEM((blocks, TILE, 3 * n), F32)] * 4 + [pltpu.VMEM((blocks, TILE, 2 * n), BF16)] * 4,
        compiler_params=pltpu.CompilerParams(vmem_limit_bytes=10 * 2**20),
        cost_estimate=pl.CostEstimate(flops=5 * 10**9, bytes_accessed=1, transcendentals=0),
        name="convolve",
    )(packed, skip, table)


def on_chip(body, shapes, *args, flops=0):
    in_vmem = pl.BlockSpec(memory_space=pltpu.VMEM)
    return pl.pallas_call(
        body,
        in_specs=[in_vmem] * len(args),
        out_specs=[in_vmem] * len(shapes),
        out_shape=[jax.ShapeDtypeStruct(shape, BF16) for shape in shapes],
        compiler_params=pltpu.CompilerParams(vmem_limit_bytes=8 * 2**20),
        cost_estimate=pl.CostEstimate(flops=flops, bytes_accessed=1, transcendentals=0),
    )(*args)


Z = 4


def project(weight, mixed, groups, rows, chunk):
    channels, tokens = mixed.shape

    def body(weight, mixed, *outs):
        me = lax.axis_index("chan")
        for pieces, out in zip(groups, outs, strict=True):
            for i, (flip, step, offset) in enumerate(pieces):
                start = ((me // Z + flip) % 2 * Z + (me % Z + step) % Z) * chunk + offset
                block = weight[pl.ds(pl.multiple_of(start, 16), rows), :]
                out[i] = jnp.dot(block, mixed[...], preferred_element_type=F32).astype(BF16)

    shapes = [(len(pieces), rows, tokens) for pieces in groups]
    total = sum(shape[0] for shape in shapes) * rows
    return on_chip(body, shapes, weight, mixed, flops=2 * total * channels * tokens)


def to_z(block, step):
    n = lax.axis_size("chan")
    return lax.ppermute(block, "chan", [(i, i // Z * Z + (i + step) % Z) for i in range(n)])


def to_x(block):
    n = lax.axis_size("chan")
    return lax.ppermute(block, "chan", [(i, (i + Z) % n) for i in range(n)])


def wide_sum(*terms):
    total = terms[0].astype(F32)
    for term in terms[1:]:
        total = total + term.astype(F32)
    return total


def add(*parts):
    arrays = [part[0] for part in parts]
    cuts = [part[1:] for part in parts]

    def body(*refs):
        refs[-1][...] = wide_sum(*(ref[a:b] for ref, (a, b) in zip(refs[:-1], cuts, strict=True))).astype(BF16)

    count = cuts[0][1] - cuts[0][0]
    (total,) = on_chip(body, [(count,) + arrays[0].shape[1:]], *arrays)
    return total


def shards(out_gate, in_gate, signal, filter_taps, skip_gain, out_proj):
    tokens, channels = out_gate.shape
    parts, chans = lax.axis_size("seq"), lax.axis_size("chan")
    per_part = channels // parts
    packed, out_gate = lax.optimization_barrier((prepare(in_gate, signal, filter_taps, parts), out_gate))

    def stage(gate, table, gate_t, staged):
        gate_t[...] = gate[...].T
        staged[...] = table[...]

    table = jnp.asarray(transform_table(tokens))
    gate_t, table = on_chip(stage, [(channels, tokens), table.shape], out_gate, table)
    packed, gate_t, table = lax.optimization_barrier((lax.all_to_all(packed, "seq", 0, 0), gate_t, table))
    skip = lax.dynamic_slice_in_dim(skip_gain, lax.axis_index("seq") * per_part, per_part, 0)
    conv = convolve(packed, skip[:, None], table)
    conv = lax.all_to_all(conv, "seq", 0, 0).reshape(channels, tokens)
    mixed = (gate_t.astype(F32) * conv.astype(F32)).astype(BF16)

    chunk = out_proj.shape[0] // chans
    half_a = 256
    half_b = chunk // 2 - half_a

    def rows_a(flip, *places):
        return [(flip, step, h * half_a) for step, h in places]

    def rows_b(*places):
        return [(flip, step, 2 * half_a + h * half_b) for step, h in places for flip in (0, 1)]

    early, late = ((2, 0), (1, 1), (2, 1), (3, 0)), ((1, 0), (3, 1), (0, 0), (0, 1))
    def run(rows, *groups):
        return project(out_proj, mixed, groups, rows, chunk)

    relay_up, relay_down = run(half_b, rows_b((2, 0)), rows_b((2, 1)))
    relay_up, relay_down, mixed = lax.optimization_barrier((relay_up, relay_down, mixed))
    relayed_up, relayed_down = to_z(relay_up, 1), to_z(relay_down, -1)
    (x_early,) = run(half_a, rows_a(1, *early))
    x_early, mixed = lax.optimization_barrier((x_early, mixed))
    x_early = to_x(x_early)
    direct_up, direct_down = run(half_b, rows_b((1, 1)), rows_b((3, 0)))
    b_below, b_above = to_z(direct_up, 1), to_z(direct_down, -1)
    (rest_b,) = run(half_b, rows_b(*late))
    (x_late,) = run(half_a, rows_a(1, *late))
    (own_a,) = run(half_a, rows_a(0, *early, *late))
    rest_b, x_late, own_a = lax.optimization_barrier((rest_b, x_late, own_a))
    x_late = to_x(x_late)

    b_up = to_z(add((rest_b, 0, 2), (relayed_up, 0, 2)), 1)
    b_down = to_z(add((rest_b, 2, 4), (relayed_down, 0, 2)), -1)

    def first_a(own, arrived, up, down):
        total = wide_sum(own[:4], arrived[...]).astype(BF16)
        up[...] = total[:2]
        down[...] = total[2:]

    up, down = on_chip(first_a, [(2, half_a, tokens)] * 2, own_a, x_early)
    a_below, a_above = to_z(up, 1), to_z(down, -1)
    a_up = to_z(add((own_a, 4, 5), (x_late, 0, 1), (a_below, 0, 1)), 1)
    a_down = to_z(add((own_a, 5, 6), (x_late, 1, 2), (a_above, 0, 1)), -1)

    def reduced_b(flip, rest, below, above, up, down):
        first = wide_sum(rest[4 + flip], above[flip], up[flip])
        second = wide_sum(rest[6 + flip], below[flip], down[flip])
        return jnp.concatenate([first, second], axis=0)

    def third_b(*refs):
        refs[-1][...] = reduced_b(1, *refs[:-1]).astype(BF16)

    (x_last,) = on_chip(third_b, [(2 * half_b, tokens)], rest_b, b_below, b_above, b_up, b_down)
    x_last = to_x(x_last)

    def last(own, x_late, below, above, up, down, x_last, rest, b_below, b_above, b_up, b_down, out, all_rows):
        first = wide_sum(own[6], x_late[2], above[1], up[0])
        second = wide_sum(own[7], x_late[3], below[1], down[0])
        all_rows[:half_a] = first.astype(BF16)
        all_rows[half_a : 2 * half_a] = second.astype(BF16)
        b_rows = reduced_b(0, rest, b_below, b_above, b_up, b_down) + x_last[...].astype(F32)
        all_rows[2 * half_a :] = b_rows.astype(BF16)
        out[...] = all_rows[...].T

    out, _ = on_chip(
        last, [(tokens, chunk), (chunk, tokens)], own_a, x_late, a_below, a_above, a_up, a_down,
        x_last, rest_b, b_below, b_above, b_up, b_down,
    )
    return out


def solution(mesh):
    return jax.shard_map(
        shards,
        mesh=mesh,
        in_specs=(
            P("seq", "chan"),
            P("seq", "chan"),
            P("seq", "chan"),
            P("seq", "chan"),
            P("chan"),
            P(None, "chan"),
        ),
        out_specs=P("seq", "chan"),
        check_vma=False,
    )
```
